256 devices in a mesh: row: 16 (over z, core), col: 16 (over y, x).
Axes of the slice: x: 4, y: 4, z: 8, core: 2. Of those that a mesh axis runs over, the one named last changes fastest.
Arguments:
- gradient: bfloat16 [8192, 26624], P('row', 'col'), may hold values from -128 to 128
- momentum: bfloat16 [8192, 26624], P('row', 'col'), may hold values from -6 to 6
- weight: bfloat16 [8192, 26624], P('row', 'col'), may hold values from -6 to 6
- right_factor: float32 [26624, 256], P('col'), may hold values from -6 to 6
Outputs:
- new_weight: bfloat16 [8192, 26624], P('row', 'col')
- new_momentum: bfloat16 [8192, 26624], P('row', 'col')
- new_factor: float32 [26624, 256], P('col')
The draws below stay inside these ranges and needn't reach their ends.
All inputs are finite; a program needn't handle non-finite values.
Results may differ from the reference program's by a relative error of at most 0.0015.
Values sent between devices are 32-bit elements; how exact they have to be, the bound alone decides.
No kernel may reach another device: no remote copies, remote signals or barrier semaphores. Data moves between devices by JAX's collectives and lax.ppermute only.
A program may use at most 64 MiB of HBM per device.

```python
import math
import jax
import jax.numpy as jnp
from jax import lax

ROWS = 8192
COLS = 26624
RANK = 256


def draw_gradient(key, part):
    key = jax.random.fold_in(key, 11)
    keys = jax.random.split(key, 7)
    row_scale = jnp.exp(jax.random.uniform(keys[0], (ROWS, 1), jnp.float32, math.log(0.3), math.log(3.0)))
    col_index = jnp.arange(COLS, dtype=jnp.float32)[None, :]
    col_scale = jnp.exp(jax.random.uniform(keys[1], (1, COLS), jnp.float32, math.log(0.5), math.log(2.0)) + math.log(3.0) * col_index / COLS)
    factors = max(RANK // 4, 1)
    base = jax.random.truncated_normal(keys[2], -4.0, 4.0, (ROWS, COLS), jnp.float32)
    row_vectors = jax.random.truncated_normal(keys[5], -4.0, 4.0, (ROWS, factors), jnp.float32)
    col_vectors = jax.random.truncated_normal(keys[6], -4.0, 4.0, (factors, COLS), jnp.float32)
    strength = 3.0
    lowrank = jnp.dot(row_vectors, col_vectors, precision=lax.Precision.HIGHEST) * (strength / math.sqrt(factors))
    return jnp.clip((base + lowrank) * row_scale * col_scale, -128.0, 128.0).astype(jnp.bfloat16)


def levels(rng, dims, pieces, low, top_value):
    def one(axis_at, parts):
        steps = jax.random.uniform(jax.random.fold_in(jax.random.fold_in(rng, 6), axis_at), (parts,), jnp.float32, low / len(pieces), top_value / len(pieces))
        return jnp.repeat(jnp.exp(steps), dims[axis_at] // parts).reshape((-1,) + (1,) * (len(dims) - axis_at - 1))

    level = one(*pieces[0])
    for cut in pieces[1:]:
        level = level * one(*cut)
    return level


def centred(rng, extent, scale, most, pieces=(), kind=jnp.bfloat16):
    gain = levels(rng, extent, pieces, -0.22, 0.18) if pieces else 1.0
    drawn = jax.random.normal(rng, extent, jnp.float32) * scale * gain
    return jnp.minimum(jnp.maximum(drawn, -most), most).astype(kind)


def setup_inputs(seed: int = 0) -> dict:
    key_list = jax.random.split(jax.random.key(seed), 5)
    gradient = draw_gradient(jax.random.fold_in(key_list[4], 71), 0)
    momentum = centred(key_list[1], (ROWS, COLS), 1.0, 6.0, ((0, 16), (1, 16)))
    weight = centred(key_list[2], (ROWS, COLS), 1.0, 6.0, ((0, 16), (1, 16)))
    right_factor = centred(key_list[3], (COLS, RANK), 1.0, 6.0, ((0, 16),), jnp.float32)
    return dict(gradient=gradient, momentum=momentum, weight=weight, right_factor=right_factor)


decay = 0.95
step_size = 0.3

def factor_gram(gram):
    jitter = 1e-06 * jnp.trace(gram) / RANK
    return jnp.linalg.cholesky(gram + jitter * jnp.eye(RANK, dtype=jnp.float32))

def solve_right(block, chol):
    return lax.linalg.triangular_solve(chol, block, left_side=False, lower=True, transpose_a=True)

def reference(gradient, momentum, weight, right_factor):
    high = lax.Precision.HIGHEST
    buffer = momentum.astype(jnp.float32) + gradient.astype(jnp.float32)
    left = jnp.dot(buffer, right_factor, precision=high)
    gram = jnp.dot(left.T, left, precision=high)
    chol = factor_gram(gram)
    ortho = solve_right(left, chol)
    right = lax.dot_general(buffer, ortho, (((0,), (0,)), ((), ())), precision=high)
    new_momentum = (buffer - (1.0 - decay) * jnp.dot(ortho, right.T, precision=high)).astype(jnp.bfloat16)
    squares = lax.optimization_barrier(jnp.sum(right * right, axis=0))
    new_factor = right / jnp.sqrt(squares / COLS + 1e-06)
    update = jnp.dot(ortho, new_factor.T, precision=high)
    new_weight = (weight.astype(jnp.float32) - step_size * jnp.sqrt(ROWS / RANK) * update).astype(jnp.bfloat16)
    return (new_weight, new_momentum, new_factor)
```

```python
import jax
import jax.numpy as jnp
from jax import lax
from jax.experimental import pallas as pl
from jax.experimental.pallas import tpu as pltpu
from jax.sharding import PartitionSpec as P

ROWS = 8192
COLS = 26624
RANK = 256
HIGHEST = lax.Precision.HIGHEST
HIGH = lax.Precision.HIGH

decay = 0.95
step_size = 0.3

HALF = 128
GROUPS = HALF // 8
CORE_SWAP = [(i, i ^ 1) for i in range(16)]
Z_GROUPS = [[z * 2 + c for z in range(8)] for c in range(2)]


def z_shift(k):
    return [(z * 2 + c, ((z + k) % 8) * 2 + c) for z in range(8) for c in range(2)]


def dot_nt(a, b, precision=HIGHEST):
    return lax.dot_general(
        a, b, (((1,), (1,)), ((), ())), precision=precision, preferred_element_type=jnp.float32
    )


def dot_nn(a, b, precision=HIGHEST):
    return lax.dot_general(
        a, b, (((1,), (0,)), ((), ())), precision=precision, preferred_element_type=jnp.float32
    )


def dot_tn(a, b, precision=HIGHEST):
    return lax.dot_general(
        a, b, (((0,), (0,)), ((), ())), precision=precision, preferred_element_type=jnp.float32
    )


def inverse_factor(block):
    rows = lax.broadcasted_iota(jnp.int32, (8, HALF), 0)
    lanes = lax.broadcasted_iota(jnp.int32, (8, HALF), 1)
    a = [block[8 * g : 8 * g + 8, :] for g in range(GROUPS)]
    x = [jnp.where(lanes == rows + 8 * g, 1.0, 0.0).astype(jnp.float32) for g in range(GROUPS)]
    diag = [jnp.ones((8, HALF), jnp.float32) for _ in range(GROUPS)]
    for j in range(HALF):
        g, s = divmod(j, 8)
        column = jnp.broadcast_to(a[g][:, j : j + 1], (8, HALF))
        pivot = jnp.broadcast_to(column[s : s + 1, :], (8, HALF))
        diag[g] = jnp.where(rows == s, pivot, diag[g])
        inverse = 1.0 / pivot
        a_row = jnp.broadcast_to(a[g][s : s + 1, :], (8, HALF)) * inverse
        x_row = jnp.broadcast_to(x[g][s : s + 1, :], (8, HALF)) * inverse
        if s < 7:
            below = jnp.where(rows > s, column, 0.0)
            a[g] = a[g] - below * a_row
            x[g] = x[g] - below * x_row
        for h in range(g + 1, GROUPS):
            column = jnp.broadcast_to(a[h][:, j : j + 1], (8, HALF))
            a[h] = a[h] - column * a_row
            x[h] = x[h] - column * x_row
    return jnp.concatenate([x[g] * lax.rsqrt(diag[g]) for g in range(GROUPS)], axis=0)


def first_kernel(gram_ref, jitter_ref, w_ref):
    gram = gram_ref[...]
    eye = lax.broadcasted_iota(jnp.int32, (RANK, RANK), 0) == lax.broadcasted_iota(
        jnp.int32, (RANK, RANK), 1
    )
    jitter = 1e-06 * jnp.sum(jnp.where(eye, gram, 0.0)) / RANK
    jitter_ref[...] = jnp.full((8, HALF), jitter, jnp.float32)
    rows = lax.broadcasted_iota(jnp.int32, (HALF, HALF), 0)
    lanes = lax.broadcasted_iota(jnp.int32, (HALF, HALF), 1)
    w_ref[...] = inverse_factor(gram[:HALF, :HALF] + jnp.where(rows == lanes, jitter, 0.0))


def second_kernel(gram_ref, jitter_ref, first_ref, w_ref):
    first = first_ref[...]
    rows = lax.broadcasted_iota(jnp.int32, (HALF, HALF), 0)
    lanes = lax.broadcasted_iota(jnp.int32, (HALF, HALF), 1)
    low = dot_nt(gram_ref[HALF:, :HALF], first)
    rest = gram_ref[HALF:, HALF:] + jnp.where(rows == lanes, jitter_ref[0:1, :], 0.0)
    second = inverse_factor(rest - dot_nt(low, low))
    w_ref[:HALF, :HALF] = first
    w_ref[:HALF, HALF:] = jnp.zeros((HALF, HALF), jnp.float32)
    w_ref[HALF:, :HALF] = -dot_nn(second, dot_nn(low, first))
    w_ref[HALF:, HALF:] = second


def inverse_cholesky(gram):
    jitter, first = pl.pallas_call(
        first_kernel,
        out_shape=(
            jax.ShapeDtypeStruct((8, HALF), jnp.float32),
            jax.ShapeDtypeStruct((HALF, HALF), jnp.float32),
        ),
        cost_estimate=pl.CostEstimate(flops=6000000, bytes_accessed=20000000, transcendentals=0),
    )(gram)
    return pl.pallas_call(
        second_kernel,
        out_shape=jax.ShapeDtypeStruct((RANK, RANK), jnp.float32),
        cost_estimate=pl.CostEstimate(flops=6000000, bytes_accessed=20000000, transcendentals=0),
    )(gram, jitter, first)


def exchange(pieces, axis, groups=None):
    return lax.all_to_all(pieces, axis, 0, 0, axis_index_groups=groups)


def spread(piece, axis, count):
    return exchange(jnp.broadcast_to(piece[None], (count,) + piece.shape), axis)


def gather_z(piece):
    z = lax.axis_index("row") // 2
    out = jnp.zeros((8,) + piece.shape, piece.dtype)
    out = lax.dynamic_update_slice(out, piece[None], (z, 0, 0))
    up = down = piece
    for k in range(1, 4):
        up = lax.ppermute(up, "row", z_shift(1))
        down = lax.ppermute(down, "row", z_shift(-1))
        out = lax.dynamic_update_slice(out, up[None], ((z - k) % 8, 0, 0))
        out = lax.dynamic_update_slice(out, down[None], ((z + k) % 8, 0, 0))
    half = piece.shape[0] // 2 // 8 * 8
    up = lax.ppermute(up[:half], "row", z_shift(1))
    down = lax.ppermute(down[half:], "row", z_shift(-1))
    last = jnp.concatenate([up, down], axis=0)
    return lax.dynamic_update_slice(out, last[None], ((z + 4) % 8, 0, 0))


def local(gradient, momentum, weight, right_factor):
    core = lax.axis_index("row") % 2
    buffer = momentum.astype(jnp.float32) + gradient.astype(jnp.float32)
    partial = dot_nn(buffer, right_factor)
    piece = jnp.sum(exchange(partial.reshape(16, 32, RANK), "col"), axis=0)
    left = spread(piece, "col", 16).reshape(512, RANK)
    gram_part = dot_tn(left, left)
    y_part = dot_tn(buffer, left)
    both = jnp.concatenate(
        [y_part.reshape(2, 8, 104, RANK), gram_part.reshape(2, 8, 16, RANK)], axis=2
    )
    mine = lax.dynamic_index_in_dim(both, core, 0, keepdims=False)
    other = lax.dynamic_index_in_dim(both, 1 - core, 0, keepdims=False)
    mine = mine + lax.ppermute(other, "row", CORE_SWAP)
    mine = jnp.sum(exchange(mine, "row", Z_GROUPS), axis=0)
    gram = spread(mine[104:], "row", 16).reshape(8, 2, 16, RANK)
    gram = jnp.transpose(gram, (1, 0, 2, 3)).reshape(RANK, RANK)
    inverse = inverse_cholesky(gram)
    y_mine = gather_z(mine[:104]).reshape(832, RANK)
    y_other = lax.ppermute(y_mine, "row", CORE_SWAP)
    y = jnp.zeros((1664, RANK), jnp.float32)
    y = lax.dynamic_update_slice(y, y_mine, (core * 832, 0))
    y = lax.dynamic_update_slice(y, y_other, ((1 - core) * 832, 0))
    right = dot_nt(y, inverse)
    ortho = dot_nt(left, inverse)
    squares = jnp.sum(spread(jnp.sum(right * right, axis=0, keepdims=True), "col", 16), axis=(0, 1))
    new_momentum = (buffer - (1.0 - decay) * dot_nt(ortho, right, HIGH)).astype(jnp.bfloat16)
    new_factor = right / jnp.sqrt(squares / COLS + 1e-06)
    update = dot_nt(ortho, new_factor, HIGH)
    new_weight = (weight.astype(jnp.float32) - step_size * jnp.sqrt(ROWS / RANK) * update).astype(
        jnp.bfloat16
    )
    return (new_weight, new_momentum, new_factor)


def solution(mesh):
    in_specs = (P("row", "col"), P("row", "col"), P("row", "col"), P("col", None))
    out_specs = (P("row", "col"), P("row", "col"), P("col", None))
    return jax.shard_map(local, mesh=mesh, in_specs=in_specs, out_specs=out_specs, check_vma=False)
```

```python
import jax
import jax.numpy as jnp
from jax import lax
from jax.experimental import pallas as pl
from jax.experimental.pallas import tpu as pltpu
from jax.sharding import PartitionSpec as P

ROWS = 8192
COLS = 26624
RANK = 256
HIGHEST = lax.Precision.HIGHEST
HIGH = lax.Precision.HIGH

decay = 0.95
step_size = 0.3

HALF = 128
GROUPS = HALF // 8
CORE_SWAP = [(i, i ^ 1) for i in range(16)]
Z_GROUPS = [[z * 2 + c for z in range(8)] for c in range(2)]


def dot_nt(a, b, precision=HIGHEST):
    return lax.dot_general(
        a, b, (((1,), (1,)), ((), ())), precision=precision, preferred_element_type=jnp.float32
    )


def dot_nn(a, b, precision=HIGHEST):
    return lax.dot_general(
        a, b, (((1,), (0,)), ((), ())), precision=precision, preferred_element_type=jnp.float32
    )


def dot_tn(a, b, precision=HIGHEST):
    return lax.dot_general(
        a, b, (((0,), (0,)), ((), ())), precision=precision, preferred_element_type=jnp.float32
    )


def inverse_factor(block):
    rows = lax.broadcasted_iota(jnp.int32, (8, HALF), 0)
    lanes = lax.broadcasted_iota(jnp.int32, (8, HALF), 1)
    a = [block[8 * g : 8 * g + 8, :] for g in range(GROUPS)]
    x = [jnp.where(lanes == rows + 8 * g, 1.0, 0.0).astype(jnp.float32) for g in range(GROUPS)]

    def lane(value, j):
        return jnp.broadcast_to(value[:, j : j + 1], (8, HALF))

    def row(value, s):
        return jnp.broadcast_to(value[s : s + 1, :], (8, HALF))

    done = []
    for g in range(GROUPS):
        columns = [lane(a[g], 8 * g + t) for t in range(8)]
        d = {(s, t): row(columns[t], s) for s in range(8) for t in range(s + 1)}
        a_rows = [row(a[g], t) for t in range(8)]
        x_rows = [row(x[g], t) for t in range(8)]
        inverse = []
        scale = jnp.ones((8, HALF), jnp.float32)
        for k in range(8):
            inverse.append(1.0 / d[k, k])
            scale = jnp.where(rows == k, d[k, k], scale)
            raw = [d.get((s, k)) for s in range(8)]
            for s in range(k + 1, 8):
                ratio = raw[s] * inverse[k]
                for t in range(k + 1, s + 1):
                    d[s, t] = d[s, t] - ratio * raw[t]
                a_rows[s] = a_rows[s] - ratio * a_rows[k]
                x_rows[s] = x_rows[s] - ratio * x_rows[k]
                d[s, k] = ratio
        final = x_rows[0]
        for s in range(1, 8):
            final = jnp.where(rows == s, x_rows[s], final)
        root = lax.rsqrt(scale)
        root = root * (1.5 - 0.5 * scale * root * root)
        done.append(final * root)
        if g == GROUPS - 1:
            break
        for t in range(7, -1, -1):
            a_rows[t] = a_rows[t] * inverse[t]
            x_rows[t] = x_rows[t] * inverse[t]
            for s in range(t + 1, 8):
                a_rows[t] = a_rows[t] - d[s, t] * a_rows[s]
                x_rows[t] = x_rows[t] - d[s, t] * x_rows[s]
        for h in range(g + 1, GROUPS):
            columns = [lane(a[h], 8 * g + t) for t in range(8)]
            for t in range(8):
                a[h] = a[h] - columns[t] * a_rows[t]
                x[h] = x[h] - columns[t] * x_rows[t]
    return jnp.concatenate(done, axis=0)


def first_kernel(col_ref, gather_ref, jitter_ref, w_ref, gram_ref):
    for k in range(16):
        gram_ref[16 * k : 16 * k + 16, :] = gather_ref[col_ref[0] ^ k]
    gram = gram_ref[...]
    eye = lax.broadcasted_iota(jnp.int32, (RANK, RANK), 0) == lax.broadcasted_iota(
        jnp.int32, (RANK, RANK), 1
    )
    jitter = 1e-06 * jnp.sum(jnp.where(eye, gram, 0.0)) / RANK
    jitter_ref[...] = jnp.full((8, HALF), jitter, jnp.float32)
    rows = lax.broadcasted_iota(jnp.int32, (HALF, HALF), 0)
    lanes = lax.broadcasted_iota(jnp.int32, (HALF, HALF), 1)
    w_ref[...] = inverse_factor(gram[:HALF, :HALF] + jnp.where(rows == lanes, jitter, 0.0))


def second_kernel(gram_ref, jitter_ref, first_ref, left_ref, w_ref, ortho_ref):
    first = first_ref[...]
    rows = lax.broadcasted_iota(jnp.int32, (HALF, HALF), 0)
    lanes = lax.broadcasted_iota(jnp.int32, (HALF, HALF), 1)
    low = dot_nt(gram_ref[HALF:, :HALF], first)
    rest = gram_ref[HALF:, HALF:] + jnp.where(rows == lanes, jitter_ref[0:1, :], 0.0)
    second = inverse_factor(rest - dot_nt(low, low))
    w_ref[:HALF, :HALF] = first
    w_ref[:HALF, HALF:] = jnp.zeros((HALF, HALF), jnp.float32)
    w_ref[HALF:, :HALF] = -dot_nn(second, dot_nn(low, first))
    w_ref[HALF:, HALF:] = second
    ortho_ref[...] = dot_nt(left_ref[...], w_ref[...])


def first_part(col, gather):
    vmem = pl.BlockSpec(memory_space=pltpu.VMEM)
    return pl.pallas_call(
        first_kernel,
        in_specs=[pl.BlockSpec(memory_space=pltpu.SMEM), vmem],
        out_specs=(vmem, vmem, vmem),
        out_shape=(
            jax.ShapeDtypeStruct((8, HALF), jnp.float32),
            jax.ShapeDtypeStruct((HALF, HALF), jnp.float32),
            jax.ShapeDtypeStruct((RANK, RANK), jnp.float32),
        ),
        cost_estimate=pl.CostEstimate(flops=6000000, bytes_accessed=20000000, transcendentals=0),
        name="first_factor",
    )(col, gather)


def second_part(jitter, first, gram, left):
    return pl.pallas_call(
        second_kernel,
        out_shape=(
            jax.ShapeDtypeStruct((RANK, RANK), jnp.float32),
            jax.ShapeDtypeStruct(left.shape, jnp.float32),
        ),
        cost_estimate=pl.CostEstimate(flops=6000000, bytes_accessed=24000000, transcendentals=0),
        name="second_factor",
    )(gram, jitter, first, left)


def halves(value):
    high = value.astype(jnp.bfloat16)
    return high, (value - high.astype(jnp.float32)).astype(jnp.bfloat16)


def product(a, b):
    return jnp.dot(a, b, preferred_element_type=jnp.float32)


def params(mib=40):
    return pltpu.CompilerParams(vmem_limit_bytes=mib * 1024 * 1024)


def left_kernel(m_ref, g_ref, r_ref, out_ref, high_ref, low_ref):
    @pl.when(pl.program_id(0) == 0)
    def _():
        high_ref[...], low_ref[...] = halves(r_ref[...])

    both = jnp.concatenate([m_ref[...], g_ref[...]], axis=0)
    total = product(both, high_ref[...]) + product(both, low_ref[...])
    count = m_ref.shape[0]
    out_ref[...] = total[:count] + total[count:]


def left_part(momentum, gradient, right_factor):
    rows, columns = momentum.shape
    step = rows // 2
    block = pl.BlockSpec((step, columns), lambda i: (i, 0))
    return pl.pallas_call(
        left_kernel,
        grid=(2,),
        in_specs=[block, block, pl.BlockSpec((columns, RANK), lambda i: (0, 0))],
        out_specs=pl.BlockSpec((step, RANK), lambda i: (i, 0)),
        out_shape=jax.ShapeDtypeStruct((rows, RANK), jnp.float32),
        scratch_shapes=[pltpu.VMEM((columns, RANK), jnp.bfloat16)] * 2,
        compiler_params=params(60),
        cost_estimate=pl.CostEstimate(flops=1744830464, bytes_accessed=5600000, transcendentals=0),
        name="left_part",
    )(momentum, gradient, right_factor)


def cross_kernel(core_ref, left_ref, m_ref, g_ref, mine_ref, other_ref, lhs_ref):
    turned = left_ref[...].T
    top, bottom = turned[:HALF], turned[HALF:]
    first = core_ref[0] == 0
    own = jnp.where(first, top, bottom)
    far = jnp.where(first, bottom, top)
    lhs_ref[0:HALF], lhs_ref[2 * HALF : 3 * HALF] = halves(own)
    lhs_ref[HALF : 2 * HALF], lhs_ref[3 * HALF :] = halves(far)
    columns = m_ref.shape[1]
    for start in range(0, columns, 256):
        stop = min(start + 256, columns)
        total = product(lhs_ref[...], m_ref[:, start:stop]) + product(lhs_ref[...], g_ref[:, start:stop])
        total = total[: 2 * HALF] + total[2 * HALF :]
        mine_ref[:, start:stop] = total[:HALF]
        other_ref[:, start:stop] = total[HALF:]


def cross_part(core, left, momentum, gradient):
    rows, columns = momentum.shape
    vmem = pl.BlockSpec(memory_space=pltpu.VMEM)
    return pl.pallas_call(
        cross_kernel,
        in_specs=[pl.BlockSpec(memory_space=pltpu.SMEM), vmem, vmem, vmem],
        out_specs=(vmem, vmem),
        out_shape=(jax.ShapeDtypeStruct((HALF, columns), jnp.float32),) * 2,
        scratch_shapes=[pltpu.VMEM((2 * RANK, rows), jnp.bfloat16)],
        compiler_params=params(),
        cost_estimate=pl.CostEstimate(flops=1744830464, bytes_accessed=5600000, transcendentals=0),
        name="cross_part",
    )(core, left, momentum, gradient)


def right_kernel(core_ref, w_ref, mine_ref, other_ref, right_ref, squares_ref):
    w = w_ref[...]
    whole = jnp.zeros((RANK, HALF), jnp.float32)
    first = core_ref[0] == 0
    columns = mine_ref.shape[1]
    for start in range(0, columns, 256):
        stop = min(start + 256, columns)
        mine, other = mine_ref[:, start:stop], other_ref[:, start:stop]
        y = jnp.concatenate([jnp.where(first, mine, other), jnp.where(first, other, mine)], axis=0)
        right = dot_nn(w, y)
        right_ref[:, start:stop] = right
        square = right * right
        for k in range(0, stop - start, HALF):
            whole = whole + square[:, k : k + HALF]
    squares_ref[...] = jnp.sum(whole.T, axis=0, keepdims=True)


def right_part(core, w, mine, other):
    columns = mine.shape[1]
    vmem = pl.BlockSpec(memory_space=pltpu.VMEM)
    return pl.pallas_call(
        right_kernel,
        in_specs=[pl.BlockSpec(memory_space=pltpu.SMEM), vmem, vmem, vmem],
        out_specs=(vmem, vmem),
        out_shape=(
            jax.ShapeDtypeStruct((RANK, columns), jnp.float32),
            jax.ShapeDtypeStruct((1, RANK), jnp.float32),
        ),
        compiler_params=params(60),
        cost_estimate=pl.CostEstimate(flops=1300000000, bytes_accessed=3400000, transcendentals=0),
        name="right_part",
    )(core, w, mine, other)


def low_rank(ortho, high_ref, low_ref, start, stop):
    count = ortho.shape[0] // 2
    total = product(ortho, high_ref[:, start:stop])
    return total[:count] + total[count:] + product(ortho[:count], low_ref[:, start:stop])


def momentum_kernel(m_ref, g_ref, ortho_ref, right_ref, out_ref, turned_ref, high_ref, low_ref):
    columns = right_ref.shape[1]

    @pl.when(pl.program_id(0) == 0)
    def _():
        for start in range(0, columns, HALF):
            block = right_ref[:, start : start + HALF]
            high_ref[:, start : start + HALF], low_ref[:, start : start + HALF] = halves(block)
            turned_ref[start : start + HALF, :] = block.T

    ortho = jnp.concatenate(halves(ortho_ref[...]), axis=0)
    for start in range(0, columns, 256):
        stop = min(start + 256, columns)
        buffer = m_ref[:, start:stop].astype(jnp.float32) + g_ref[:, start:stop].astype(jnp.float32)
        update = low_rank(ortho, high_ref, low_ref, start, stop)
        out_ref[:, start:stop] = (buffer - (1.0 - decay) * update).astype(jnp.bfloat16)


def momentum_part(momentum, gradient, ortho, right):
    rows, columns = momentum.shape
    step = rows // 4
    block = pl.BlockSpec((step, columns), lambda i: (i, 0))
    wide = pl.BlockSpec((RANK, columns), lambda i: (0, 0))
    return pl.pallas_call(
        momentum_kernel,
        grid=(4,),
        in_specs=[block, block, pl.BlockSpec((step, RANK), lambda i: (i, 0)), wide],
        out_specs=(block, pl.BlockSpec((columns, RANK), lambda i: (0, 0)), wide, wide),
        out_shape=(
            jax.ShapeDtypeStruct((rows, columns), jnp.bfloat16),
            jax.ShapeDtypeStruct((columns, RANK), jnp.float32),
            jax.ShapeDtypeStruct((RANK, columns), jnp.bfloat16),
            jax.ShapeDtypeStruct((RANK, columns), jnp.bfloat16),
        ),
        compiler_params=params(60),
        cost_estimate=pl.CostEstimate(flops=1308622848, bytes_accessed=7500000, transcendentals=0),
        name="momentum_part",
    )(momentum, gradient, ortho, right)


def weight_kernel(squares_ref, weight_ref, ortho_ref, turned_ref, high_ref, low_ref, out_ref, factor_ref):
    squares = jnp.sum(squares_ref[...], axis=0, keepdims=True)
    scale = 1.0 / jnp.sqrt(squares / COLS + 1e-06)
    rate = step_size * (ROWS / RANK) ** 0.5
    ortho = jnp.concatenate(halves(ortho_ref[...] * (scale * rate)), axis=0)
    columns = high_ref.shape[1]
    for start in range(0, columns, 256):
        stop = min(start + 256, columns)
        update = low_rank(ortho, high_ref, low_ref, start, stop)
        out_ref[:, start:stop] = (weight_ref[:, start:stop].astype(jnp.float32) - update).astype(
            jnp.bfloat16
        )
    factor_ref[...] = turned_ref[...] * scale


def weight_part(squares, weight, ortho, turned, high, low):
    rows, columns = weight.shape
    step = rows // 4
    block = pl.BlockSpec((step, columns), lambda i: (i, 0))
    wide = pl.BlockSpec((RANK, columns), lambda i: (0, 0))
    factor = pl.BlockSpec((columns // 4, RANK), lambda i: (i, 0))
    return pl.pallas_call(
        weight_kernel,
        grid=(4,),
        in_specs=[
            pl.BlockSpec((16, RANK), lambda i: (0, 0)),
            block,
            pl.BlockSpec((step, RANK), lambda i: (i, 0)),
            factor,
            wide,
            wide,
        ],
        out_specs=(block, factor),
        out_shape=(
            jax.ShapeDtypeStruct((rows, columns), jnp.bfloat16),
            jax.ShapeDtypeStruct((columns, RANK), jnp.float32),
        ),
        compiler_params=params(60),
        cost_estimate=pl.CostEstimate(flops=1308622848, bytes_accessed=7500000, transcendentals=0),
        name="weight_part",
    )(squares, weight, ortho, turned, high, low)


def exchange(pieces, axis, groups=None):
    return lax.all_to_all(pieces, axis, 0, 0, axis_index_groups=groups)


def spread(piece, axis, count, groups=None):
    return exchange(jnp.broadcast_to(piece[None], (count,) + piece.shape), axis, groups)


def gather_col(piece):
    out = piece[None]
    for bit in (1, 2, 4, 8):
        pairs = [(i, i ^ bit) for i in range(16)]
        out = jnp.concatenate([out, lax.ppermute(out, "col", pairs)], axis=0)
    return out


def local(gradient, momentum, weight, right_factor):
    core = (lax.axis_index("row") % 2).reshape(1)
    col = lax.axis_index("col")
    partial = left_part(momentum, gradient, right_factor)
    piece = jnp.sum(exchange(partial.reshape(16, 32, RANK), "col"), axis=0)
    left = spread(piece, "col", 16).reshape(512, RANK)
    gram = dot_tn(lax.dynamic_slice(left, (0, col * 16), (512, 16)), left)
    gram = jnp.sum(spread(gram, "row", 16), axis=0)
    mine, other = cross_part(core, left, momentum, gradient)
    gram, other = lax.optimization_barrier((gram, other))
    mine = mine + lax.ppermute(other, "row", CORE_SWAP)
    mine = jnp.sum(exchange(mine.reshape(8, 16, 1664), "row", Z_GROUPS), axis=0)
    jitter, first, gram = first_part(col.reshape(1), gather_col(gram))
    mine, first = lax.optimization_barrier((mine, first))
    inverse, ortho = second_part(jitter, first, gram, left)
    mine = spread(mine, "row", 8, Z_GROUPS).reshape(HALF, 1664)
    mine, inverse = lax.optimization_barrier((mine, inverse))
    other = lax.ppermute(mine, "row", CORE_SWAP)
    right, squares = right_part(core, inverse, mine, other)
    squares = spread(squares, "col", 16).reshape(16, RANK)
    new_momentum, turned, high, low = momentum_part(momentum, gradient, ortho, right)
    new_weight, new_factor = weight_part(squares, weight, ortho, turned, high, low)
    return (new_weight, new_momentum, new_factor)


def solution(mesh):
    in_specs = (P("row", "col"), P("row", "col"), P("row", "col"), P("col", None))
    out_specs = (P("row", "col"), P("row", "col"), P("col", None))
    return jax.shard_map(local, mesh=mesh, in_specs=in_specs, out_specs=out_specs, check_vma=False)
```

```python
import jax
import jax.numpy as jnp
from jax import lax
from jax.experimental import pallas as pl
from jax.experimental.pallas import tpu as pltpu
from jax.sharding import PartitionSpec as P

ROWS = 8192
COLS = 26624
RANK = 256
HIGHEST = lax.Precision.HIGHEST
HIGH = lax.Precision.HIGH

decay = 0.95
step_size = 0.3

HALF = 128
GROUPS = HALF // 8
CORE_SWAP = [(i, i ^ 1) for i in range(16)]
Z_GROUPS = [[z * 2 + c for z in range(8)] for c in range(2)]


def dot_nt(a, b, precision=HIGHEST):
    return lax.dot_general(
        a, b, (((1,), (1,)), ((), ())), precision=precision, preferred_element_type=jnp.float32
    )


def dot_nn(a, b, precision=HIGHEST):
    return lax.dot_general(
        a, b, (((1,), (0,)), ((), ())), precision=precision, preferred_element_type=jnp.float32
    )


def dot_tn(a, b, precision=HIGHEST):
    return lax.dot_general(
        a, b, (((0,), (0,)), ((), ())), precision=precision, preferred_element_type=jnp.float32
    )


def inverse_factor(block):
    rows = lax.broadcasted_iota(jnp.int32, (8, HALF), 0)
    lanes = lax.broadcasted_iota(jnp.int32, (8, HALF), 1)
    a = [block[8 * g : 8 * g + 8, :] for g in range(GROUPS)]
    x = [jnp.where(lanes == rows + 8 * g, 1.0, 0.0).astype(jnp.float32) for g in range(GROUPS)]

    def lane(value, j):
        return jnp.broadcast_to(value[:, j : j + 1], (8, HALF))

    def row(value, s):
        return jnp.broadcast_to(value[s : s + 1, :], (8, HALF))

    done = []
    for g in range(GROUPS):
        columns = [lane(a[g], 8 * g + t) for t in range(8)]
        d = {(s, t): row(columns[t], s) for s in range(8) for t in range(s + 1)}
        a_rows = [row(a[g], t) for t in range(8)]
        x_rows = [row(x[g], t) for t in range(8)]
        inverse = []
        scale = jnp.ones((8, HALF), jnp.float32)
        for k in range(8):
            inverse.append(1.0 / d[k, k])
            scale = jnp.where(rows == k, d[k, k], scale)
            raw = [d.get((s, k)) for s in range(8)]
            for s in range(k + 1, 8):
                ratio = raw[s] * inverse[k]
                for t in range(k + 1, s + 1):
                    d[s, t] = d[s, t] - ratio * raw[t]
                a_rows[s] = a_rows[s] - ratio * a_rows[k]
                x_rows[s] = x_rows[s] - ratio * x_rows[k]
                d[s, k] = ratio
        final = x_rows[0]
        for s in range(1, 8):
            final = jnp.where(rows == s, x_rows[s], final)
        root = lax.rsqrt(scale)
        root = root * (1.5 - 0.5 * scale * root * root)
        done.append(final * root)
        if g == GROUPS - 1:
            break
        for t in range(7, -1, -1):
            a_rows[t] = a_rows[t] * inverse[t]
            x_rows[t] = x_rows[t] * inverse[t]
            for s in range(t + 1, 8):
                a_rows[t] = a_rows[t] - d[s, t] * a_rows[s]
                x_rows[t] = x_rows[t] - d[s, t] * x_rows[s]
        for h in range(g + 1, GROUPS):
            columns = [lane(a[h], 8 * g + t) for t in range(8)]
            for t in range(8):
                a[h] = a[h] - columns[t] * a_rows[t]
                x[h] = x[h] - columns[t] * x_rows[t]
    return jnp.concatenate(done, axis=0)


def first_kernel(col_ref, gather_ref, jitter_ref, w_ref, gram_ref):
    for k in range(16):
        gram_ref[16 * k : 16 * k + 16, :] = gather_ref[col_ref[0] ^ k]
    gram = gram_ref[...]
    eye = lax.broadcasted_iota(jnp.int32, (RANK, RANK), 0) == lax.broadcasted_iota(
        jnp.int32, (RANK, RANK), 1
    )
    jitter = 1e-06 * jnp.sum(jnp.where(eye, gram, 0.0)) / RANK
    jitter_ref[...] = jnp.full((8, HALF), jitter, jnp.float32)
    rows = lax.broadcasted_iota(jnp.int32, (HALF, HALF), 0)
    lanes = lax.broadcasted_iota(jnp.int32, (HALF, HALF), 1)
    w_ref[...] = inverse_factor(gram[:HALF, :HALF] + jnp.where(rows == lanes, jitter, 0.0))


def second_kernel(gram_ref, jitter_ref, first_ref, left_ref, w_ref, ortho_ref):
    first = first_ref[...]
    rows = lax.broadcasted_iota(jnp.int32, (HALF, HALF), 0)
    lanes = lax.broadcasted_iota(jnp.int32, (HALF, HALF), 1)
    low = dot_nt(gram_ref[HALF:, :HALF], first)
    rest = gram_ref[HALF:, HALF:] + jnp.where(rows == lanes, jitter_ref[0:1, :], 0.0)
    second = inverse_factor(rest - dot_nt(low, low))
    w_ref[:HALF, :HALF] = first
    w_ref[:HALF, HALF:] = jnp.zeros((HALF, HALF), jnp.float32)
    w_ref[HALF:, :HALF] = -dot_nn(second, dot_nn(low, first))
    w_ref[HALF:, HALF:] = second
    ortho_ref[...] = dot_nt(left_ref[...], w_ref[...])


def first_part(col, gather):
    vmem = pl.BlockSpec(memory_space=pltpu.VMEM)
    return pl.pallas_call(
        first_kernel,
        in_specs=[pl.BlockSpec(memory_space=pltpu.SMEM), vmem],
        out_specs=(vmem, vmem, vmem),
        out_shape=(
            jax.ShapeDtypeStruct((8, HALF), jnp.float32),
            jax.ShapeDtypeStruct((HALF, HALF), jnp.float32),
            jax.ShapeDtypeStruct((RANK, RANK), jnp.float32),
        ),
        cost_estimate=pl.CostEstimate(flops=6000000, bytes_accessed=20000000, transcendentals=0),
        name="first_factor",
    )(col, gather)


def second_part(jitter, first, gram, left):
    return pl.pallas_call(
        second_kernel,
        out_shape=(
            jax.ShapeDtypeStruct((RANK, RANK), jnp.float32),
            jax.ShapeDtypeStruct(left.shape, jnp.float32),
        ),
        cost_estimate=pl.CostEstimate(flops=6000000, bytes_accessed=24000000, transcendentals=0),
        name="second_factor",
    )(gram, jitter, first, left)


def halves(value):
    high = value.astype(jnp.bfloat16)
    return high, (value - high.astype(jnp.float32)).astype(jnp.bfloat16)


def product(a, b):
    return jnp.dot(a, b, preferred_element_type=jnp.float32)


def params(mib=40):
    return pltpu.CompilerParams(vmem_limit_bytes=mib * 1024 * 1024)


def left_kernel(m_ref, g_ref, r_ref, out_ref, high_ref, low_ref):
    @pl.when(pl.program_id(0) == 0)
    def _():
        high_ref[...], low_ref[...] = halves(r_ref[...])

    both = jnp.concatenate([m_ref[...], g_ref[...]], axis=0)
    total = product(both, high_ref[...]) + product(both, low_ref[...])
    count = m_ref.shape[0]
    out_ref[...] = total[:count] + total[count:]


def left_part(momentum, gradient, right_factor):
    rows, columns = momentum.shape
    step = rows // 2
    block = pl.BlockSpec((step, columns), lambda i: (i, 0))
    return pl.pallas_call(
        left_kernel,
        grid=(2,),
        in_specs=[block, block, pl.BlockSpec((columns, RANK), lambda i: (0, 0))],
        out_specs=pl.BlockSpec((step, RANK), lambda i: (i, 0)),
        out_shape=jax.ShapeDtypeStruct((rows, RANK), jnp.float32),
        scratch_shapes=[pltpu.VMEM((columns, RANK), jnp.bfloat16)] * 2,
        compiler_params=params(60),
        cost_estimate=pl.CostEstimate(flops=1744830464, bytes_accessed=5600000, transcendentals=0),
        name="left_part",
    )(momentum, gradient, right_factor)


def cross_kernel(core_ref, left_ref, m_ref, g_ref, mine_ref, other_ref, lhs_ref):
    turned = left_ref[...].T
    top, bottom = turned[:HALF], turned[HALF:]
    first = core_ref[0] == 0
    own = jnp.where(first, top, bottom)
    far = jnp.where(first, bottom, top)
    lhs_ref[0:HALF], lhs_ref[2 * HALF : 3 * HALF] = halves(own)
    lhs_ref[HALF : 2 * HALF], lhs_ref[3 * HALF :] = halves(far)
    columns = m_ref.shape[1]
    for start in range(0, columns, 256):
        stop = min(start + 256, columns)
        total = product(lhs_ref[...], m_ref[:, start:stop]) + product(lhs_ref[...], g_ref[:, start:stop])
        total = total[: 2 * HALF] + total[2 * HALF :]
        mine_ref[:, start:stop] = total[:HALF]
        other_ref[:, start:stop] = total[HALF:]


def cross_part(core, left, momentum, gradient):
    rows, columns = momentum.shape
    vmem = pl.BlockSpec(memory_space=pltpu.VMEM)
    return pl.pallas_call(
        cross_kernel,
        in_specs=[pl.BlockSpec(memory_space=pltpu.SMEM), vmem, vmem, vmem],
        out_specs=(vmem, vmem),
        out_shape=(jax.ShapeDtypeStruct((HALF, columns), jnp.float32),) * 2,
        scratch_shapes=[pltpu.VMEM((2 * RANK, rows), jnp.bfloat16)],
        compiler_params=params(),
        cost_estimate=pl.CostEstimate(flops=1744830464, bytes_accessed=5600000, transcendentals=0),
        name="cross_part",
    )(core, left, momentum, gradient)


def right_kernel(core_ref, w_ref, mine_ref, other_ref, right_ref, squares_ref):
    w = w_ref[...]
    whole = jnp.zeros((RANK, HALF), jnp.float32)
    first = core_ref[0] == 0
    columns = mine_ref.shape[1]
    for start in range(0, columns, 256):
        stop = min(start + 256, columns)
        mine, other = mine_ref[:, start:stop], other_ref[:, start:stop]
        y = jnp.concatenate([jnp.where(first, mine, other), jnp.where(first, other, mine)], axis=0)
        right = dot_nn(w, y)
        right_ref[:, start:stop] = right
        square = right * right
        for k in range(0, stop - start, HALF):
            whole = whole + square[:, k : k + HALF]
    total = jnp.sum(whole.T, axis=0, keepdims=True)
    squares_ref[...] = jnp.broadcast_to(total[None], squares_ref.shape)


def right_part(core, w, mine, other):
    columns = mine.shape[1]
    vmem = pl.BlockSpec(memory_space=pltpu.VMEM)
    return pl.pallas_call(
        right_kernel,
        in_specs=[pl.BlockSpec(memory_space=pltpu.SMEM), vmem, vmem, vmem],
        out_specs=(vmem, vmem),
        out_shape=(
            jax.ShapeDtypeStruct((RANK, columns), jnp.float32),
            jax.ShapeDtypeStruct((16, 8, RANK), jnp.float32),
        ),
        compiler_params=params(40),
        cost_estimate=pl.CostEstimate(flops=1300000000, bytes_accessed=3400000, transcendentals=0),
        name="right_part",
    )(core, w, mine, other)


def low_rank(ortho, high_ref, low_ref, start, stop):
    count = ortho.shape[0] // 2
    total = product(ortho, high_ref[:, start:stop])
    return total[:count] + total[count:] + product(ortho[:count], low_ref[:, start:stop])


def momentum_kernel(m_ref, g_ref, ortho_ref, right_ref, out_ref, turned_ref, high_ref, low_ref):
    columns = right_ref.shape[1]

    @pl.when(pl.program_id(0) == 0)
    def _():
        for start in range(0, columns, HALF):
            block = right_ref[:, start : start + HALF]
            high_ref[:, start : start + HALF], low_ref[:, start : start + HALF] = halves(block)
            turned_ref[start : start + HALF, :] = block.T

    ortho = jnp.concatenate(halves(ortho_ref[...]), axis=0)
    for start in range(0, columns, 256):
        stop = min(start + 256, columns)
        buffer = m_ref[:, start:stop].astype(jnp.float32) + g_ref[:, start:stop].astype(jnp.float32)
        update = low_rank(ortho, high_ref, low_ref, start, stop)
        out_ref[:, start:stop] = (buffer - (1.0 - decay) * update).astype(jnp.bfloat16)


def momentum_part(momentum, gradient, ortho, right):
    rows, columns = momentum.shape
    step = rows // 4
    block = pl.BlockSpec((step, columns), lambda i: (i, 0))
    wide = pl.BlockSpec((RANK, columns), lambda i: (0, 0))
    return pl.pallas_call(
        momentum_kernel,
        grid=(4,),
        in_specs=[block, block, pl.BlockSpec((step, RANK), lambda i: (i, 0)), wide],
        out_specs=(block, pl.BlockSpec((columns, RANK), lambda i: (0, 0)), wide, wide),
        out_shape=(
            jax.ShapeDtypeStruct((rows, columns), jnp.bfloat16),
            jax.ShapeDtypeStruct((columns, RANK), jnp.float32),
            jax.ShapeDtypeStruct((RANK, columns), jnp.bfloat16),
            jax.ShapeDtypeStruct((RANK, columns), jnp.bfloat16),
        ),
        compiler_params=params(60),
        cost_estimate=pl.CostEstimate(flops=1308622848, bytes_accessed=7500000, transcendentals=0),
        name="momentum_part",
    )(momentum, gradient, ortho, right)


def weight_kernel(squares_ref, weight_ref, ortho_ref, turned_ref, high_ref, low_ref, out_ref, factor_ref):
    squares = jnp.sum(squares_ref[...], axis=0)[0:1]
    scale = 1.0 / jnp.sqrt(squares / COLS + 1e-06)
    rate = step_size * (ROWS / RANK) ** 0.5
    ortho = jnp.concatenate(halves(ortho_ref[...] * (scale * rate)), axis=0)
    columns = high_ref.shape[1]
    for start in range(0, columns, 256):
        stop = min(start + 256, columns)
        update = low_rank(ortho, high_ref, low_ref, start, stop)
        out_ref[:, start:stop] = (weight_ref[:, start:stop].astype(jnp.float32) - update).astype(
            jnp.bfloat16
        )
    factor_ref[...] = turned_ref[...] * scale


def weight_part(squares, weight, ortho, turned, high, low):
    rows, columns = weight.shape
    step = rows // 4
    block = pl.BlockSpec((step, columns), lambda i: (i, 0))
    wide = pl.BlockSpec((RANK, columns), lambda i: (0, 0))
    factor = pl.BlockSpec((columns // 4, RANK), lambda i: (i, 0))
    return pl.pallas_call(
        weight_kernel,
        grid=(4,),
        in_specs=[
            pl.BlockSpec((16, 8, RANK), lambda i: (0, 0, 0)),
            block,
            pl.BlockSpec((step, RANK), lambda i: (i, 0)),
            factor,
            wide,
            wide,
        ],
        out_specs=(block, factor),
        out_shape=(
            jax.ShapeDtypeStruct((rows, columns), jnp.bfloat16),
            jax.ShapeDtypeStruct((columns, RANK), jnp.float32),
        ),
        compiler_params=params(60),
        cost_estimate=pl.CostEstimate(flops=1308622848, bytes_accessed=7500000, transcendentals=0),
        name="weight_part",
    )(squares, weight, ortho, turned, high, low)


def exchange(pieces, axis, groups=None):
    return lax.all_to_all(pieces, axis, 0, 0, axis_index_groups=groups)


def spread(piece, axis, count, groups=None):
    return exchange(jnp.broadcast_to(piece[None], (count,) + piece.shape), axis, groups)


def swap(value, axis, bits):
    return lax.ppermute(value, axis, [(i, i ^ bits) for i in range(16)])


def z_shift(k):
    return [(z * 2 + c, ((z + k) % 8) * 2 + c) for z in range(8) for c in range(2)]


def gather_near(piece, unit):
    return jnp.concatenate([piece] + [swap(piece, "col", k * unit) for k in (1, 2, 3)], axis=0)


def scatter_z(pieces, gram):
    z = lax.axis_index("row") // 2

    def own(k):
        return lax.dynamic_index_in_dim(pieces, (z + k) % 8, 0, keepdims=False)

    down, up = own(-4), own(3)
    for k, bits in enumerate((2, 4, 14)):
        down = lax.ppermute(down, "row", z_shift(-1)) + own(k - 3)
        up = lax.ppermute(up, "row", z_shift(1))
        up = up + own(2 - k)
        gram = gram + swap(gram, "row", bits)
        down, up, gram = lax.optimization_barrier((down, up, gram))
    gram = gather_near(gram[None], 1)
    total = up + lax.ppermute(down, "row", z_shift(-1))
    return lax.optimization_barrier((total, gather_near(gram, 4)))


def local(gradient, momentum, weight, right_factor):
    core = (lax.axis_index("row") % 2).reshape(1)
    col = lax.axis_index("col")
    partial = left_part(momentum, gradient, right_factor)
    piece = jnp.sum(exchange(partial.reshape(16, 32, RANK), "col"), axis=0)
    left = spread(piece, "col", 16).reshape(512, RANK)
    gram = dot_tn(lax.dynamic_slice(left, (0, col * 16), (512, 16)), left)
    left, gram = lax.optimization_barrier((left, gram))
    gram = gram + swap(gram, "row", 1)
    mine, other = cross_part(core, left, momentum, gradient)
    mine = mine + lax.ppermute(other, "row", CORE_SWAP)
    mine, gram = lax.optimization_barrier((mine, gram))
    mine, gram = scatter_z(mine.reshape(8, 16, 1664), gram)
    mine = spread(mine, "row", 8, Z_GROUPS).reshape(HALF, 1664)
    jitter, first, gram = first_part(col.reshape(1), gram)
    inverse, ortho = second_part(jitter, first, gram, left)
    mine, inverse = lax.optimization_barrier((mine, inverse))
    other = lax.ppermute(mine, "row", CORE_SWAP)
    right, squares = right_part(core, inverse, mine, other)
    squares = exchange(squares, "col")
    new_momentum, turned, high, low = momentum_part(momentum, gradient, ortho, right)
    new_weight, new_factor = weight_part(squares, weight, ortho, turned, high, low)
    return (new_weight, new_momentum, new_factor)


def solution(mesh):
    in_specs = (P("row", "col"), P("row", "col"), P("row", "col"), P("col", None))
    out_specs = (P("row", "col"), P("row", "col"), P("col", None))
    return jax.shard_map(local, mesh=mesh, in_specs=in_specs, out_specs=out_specs, check_vma=False)
```

```python
import jax
import jax.numpy as jnp
from jax import lax
from jax.experimental import pallas as pl
from jax.experimental.pallas import tpu as pltpu
from jax.sharding import PartitionSpec as P

ROWS = 8192
COLS = 26624
RANK = 256
HIGHEST = lax.Precision.HIGHEST
HIGH = lax.Precision.HIGH

decay = 0.95
step_size = 0.3

HALF = 128
GROUPS = HALF // 8
CORE_SWAP = [(i, i ^ 1) for i in range(16)]
Z_GROUPS = [[z * 2 + c for z in range(8)] for c in range(2)]


def dot_nt(a, b, precision=HIGHEST):
    return lax.dot_general(
        a, b, (((1,), (1,)), ((), ())), precision=precision, preferred_element_type=jnp.float32
    )


def dot_nn(a, b, precision=HIGHEST):
    return lax.dot_general(
        a, b, (((1,), (0,)), ((), ())), precision=precision, preferred_element_type=jnp.float32
    )


def dot_tn(a, b, precision=HIGHEST):
    return lax.dot_general(
        a, b, (((0,), (0,)), ((), ())), precision=precision, preferred_element_type=jnp.float32
    )


def inverse_factor(block):
    rows = lax.broadcasted_iota(jnp.int32, (8, HALF), 0)
    lanes = lax.broadcasted_iota(jnp.int32, (8, HALF), 1)
    a = [block[8 * g : 8 * g + 8, :] for g in range(GROUPS)]
    x = [jnp.where(lanes == rows + 8 * g, 1.0, 0.0).astype(jnp.float32) for g in range(GROUPS)]

    def lane(value, j):
        return jnp.broadcast_to(value[:, j : j + 1], (8, HALF))

    def row(value, s):
        return jnp.broadcast_to(value[s : s + 1, :], (8, HALF))

    done = []
    for g in range(GROUPS):
        columns = [lane(a[g], 8 * g + t) for t in range(8)]
        d = {(s, t): row(columns[t], s) for s in range(8) for t in range(s + 1)}
        a_rows = [row(a[g], t) for t in range(8)]
        x_rows = [row(x[g], t) for t in range(8)]
        inverse = []
        scale = jnp.ones((8, HALF), jnp.float32)
        for k in range(8):
            inverse.append(1.0 / d[k, k])
            scale = jnp.where(rows == k, d[k, k], scale)
            raw = [d.get((s, k)) for s in range(8)]
            for s in range(k + 1, 8):
                ratio = raw[s] * inverse[k]
                for t in range(k + 1, s + 1):
                    d[s, t] = d[s, t] - ratio * raw[t]
                a_rows[s] = a_rows[s] - ratio * a_rows[k]
                x_rows[s] = x_rows[s] - ratio * x_rows[k]
                d[s, k] = ratio
        final = x_rows[0]
        for s in range(1, 8):
            final = jnp.where(rows == s, x_rows[s], final)
        root = lax.rsqrt(scale)
        root = root * (1.5 - 0.5 * scale * root * root)
        done.append(final * root)
        if g == GROUPS - 1:
            break
        for t in range(7, -1, -1):
            a_rows[t] = a_rows[t] * inverse[t]
            x_rows[t] = x_rows[t] * inverse[t]
            for s in range(t + 1, 8):
                a_rows[t] = a_rows[t] - d[s, t] * a_rows[s]
                x_rows[t] = x_rows[t] - d[s, t] * x_rows[s]
        for h in range(g + 1, GROUPS):
            columns = [lane(a[h], 8 * g + t) for t in range(8)]
            for t in range(8):
                a[h] = a[h] - columns[t] * a_rows[t]
                x[h] = x[h] - columns[t] * x_rows[t]
    return jnp.concatenate(done, axis=0)


def first_kernel(col_ref, gather_ref, jitter_ref, w_ref, gram_ref):
    for k in range(16):
        gram_ref[16 * k : 16 * k + 16, :] = gather_ref[col_ref[0] ^ k]
    gram = gram_ref[...]
    eye = lax.broadcasted_iota(jnp.int32, (RANK, RANK), 0) == lax.broadcasted_iota(
        jnp.int32, (RANK, RANK), 1
    )
    jitter = 1e-06 * jnp.sum(jnp.where(eye, gram, 0.0)) / RANK
    jitter_ref[...] = jnp.full((8, HALF), jitter, jnp.float32)
    rows = lax.broadcasted_iota(jnp.int32, (HALF, HALF), 0)
    lanes = lax.broadcasted_iota(jnp.int32, (HALF, HALF), 1)
    w_ref[...] = inverse_factor(gram[:HALF, :HALF] + jnp.where(rows == lanes, jitter, 0.0))


def second_kernel(gram_ref, jitter_ref, first_ref, left_ref, w_ref, ortho_ref):
    first = first_ref[...]
    rows = lax.broadcasted_iota(jnp.int32, (HALF, HALF), 0)
    lanes = lax.broadcasted_iota(jnp.int32, (HALF, HALF), 1)
    low = dot_nt(gram_ref[HALF:, :HALF], first)
    rest = gram_ref[HALF:, HALF:] + jnp.where(rows == lanes, jitter_ref[0:1, :], 0.0)
    second = inverse_factor(rest - dot_nt(low, low))
    w_ref[:HALF, :HALF] = first
    w_ref[:HALF, HALF:] = jnp.zeros((HALF, HALF), jnp.float32)
    w_ref[HALF:, :HALF] = -dot_nn(second, dot_nn(low, first))
    w_ref[HALF:, HALF:] = second
    ortho_ref[...] = dot_nt(left_ref[...], w_ref[...])


def first_part(col, gather):
    vmem = pl.BlockSpec(memory_space=pltpu.VMEM)
    return pl.pallas_call(
        first_kernel,
        in_specs=[pl.BlockSpec(memory_space=pltpu.SMEM), vmem],
        out_specs=(vmem, vmem, vmem),
        out_shape=(
            jax.ShapeDtypeStruct((8, HALF), jnp.float32),
            jax.ShapeDtypeStruct((HALF, HALF), jnp.float32),
            jax.ShapeDtypeStruct((RANK, RANK), jnp.float32),
        ),
        compiler_params=params(24),
        cost_estimate=pl.CostEstimate(flops=6000000, bytes_accessed=20000000, transcendentals=0),
        name="first_factor",
    )(col, gather)


def second_part(jitter, first, gram, left):
    return pl.pallas_call(
        second_kernel,
        out_shape=(
            jax.ShapeDtypeStruct((RANK, RANK), jnp.float32),
            jax.ShapeDtypeStruct(left.shape, jnp.float32),
        ),
        compiler_params=params(24),
        cost_estimate=pl.CostEstimate(flops=6000000, bytes_accessed=24000000, transcendentals=0),
        name="second_factor",
    )(gram, jitter, first, left)


def halves(value):
    high = value.astype(jnp.bfloat16)
    return high, (value - high.astype(jnp.float32)).astype(jnp.bfloat16)


def product(a, b):
    return jnp.dot(a, b, preferred_element_type=jnp.float32)


def params(mib=40):
    return pltpu.CompilerParams(vmem_limit_bytes=mib * 1024 * 1024)


def left_kernel(m_ref, g_ref, r_ref, out_ref, high_ref, low_ref):
    @pl.when(pl.program_id(0) == 0)
    def _():
        high_ref[...], low_ref[...] = halves(r_ref[...])

    both = jnp.concatenate([m_ref[...], g_ref[...]], axis=0)
    total = product(both, high_ref[...]) + product(both, low_ref[...])
    count = m_ref.shape[0]
    out_ref[...] = total[:count] + total[count:]


def left_part(momentum, gradient, right_factor):
    rows, columns = momentum.shape
    step = rows // 2
    block = pl.BlockSpec((step, columns), lambda i: (i, 0))
    return pl.pallas_call(
        left_kernel,
        grid=(2,),
        in_specs=[block, block, pl.BlockSpec((columns, RANK), lambda i: (0, 0))],
        out_specs=pl.BlockSpec((step, RANK), lambda i: (i, 0)),
        out_shape=jax.ShapeDtypeStruct((rows, RANK), jnp.float32),
        scratch_shapes=[pltpu.VMEM((columns, RANK), jnp.bfloat16)] * 2,
        compiler_params=params(60),
        cost_estimate=pl.CostEstimate(flops=1744830464, bytes_accessed=5600000, transcendentals=0),
        name="left_part",
    )(momentum, gradient, right_factor)


def cross_kernel(core_ref, left_ref, m_ref, g_ref, mine_ref, other_ref, lhs_ref):
    turned = left_ref[...].T
    top, bottom = turned[:HALF], turned[HALF:]
    first = core_ref[0] == 0
    own = jnp.where(first, top, bottom)
    far = jnp.where(first, bottom, top)
    lhs_ref[0:HALF], lhs_ref[2 * HALF : 3 * HALF] = halves(own)
    lhs_ref[HALF : 2 * HALF], lhs_ref[3 * HALF :] = halves(far)
    columns = m_ref.shape[1]
    for start in range(0, columns, 256):
        stop = min(start + 256, columns)
        total = product(lhs_ref[...], m_ref[:, start:stop]) + product(lhs_ref[...], g_ref[:, start:stop])
        total = total[: 2 * HALF] + total[2 * HALF :]
        mine_ref[:, start:stop] = total[:HALF]
        other_ref[:, start:stop] = total[HALF:]


def cross_part(core, left, momentum, gradient):
    rows, columns = momentum.shape
    vmem = pl.BlockSpec(memory_space=pltpu.VMEM)
    return pl.pallas_call(
        cross_kernel,
        in_specs=[pl.BlockSpec(memory_space=pltpu.SMEM), vmem, vmem, vmem],
        out_specs=(vmem, vmem),
        out_shape=(jax.ShapeDtypeStruct((HALF, columns), jnp.float32),) * 2,
        scratch_shapes=[pltpu.VMEM((2 * RANK, rows), jnp.bfloat16)],
        compiler_params=params(),
        cost_estimate=pl.CostEstimate(flops=1744830464, bytes_accessed=5600000, transcendentals=0),
        name="cross_part",
    )(core, left, momentum, gradient)


def right_kernel(core_ref, w_ref, mine_ref, other_ref, right_ref, squares_ref):
    w = w_ref[...]
    whole = jnp.zeros((RANK, HALF), jnp.float32)
    first = core_ref[0] == 0
    columns = mine_ref.shape[1]
    for start in range(0, columns, 256):
        stop = min(start + 256, columns)
        mine, other = mine_ref[:, start:stop], other_ref[:, start:stop]
        y = jnp.concatenate([jnp.where(first, mine, other), jnp.where(first, other, mine)], axis=0)
        right = dot_nn(w, y)
        right_ref[:, start:stop] = right
        square = right * right
        for k in range(0, stop - start, HALF):
            whole = whole + square[:, k : k + HALF]
    total = jnp.sum(whole.T, axis=0, keepdims=True)
    squares_ref[...] = jnp.broadcast_to(total[None], squares_ref.shape)


def right_part(core, w, mine, other):
    columns = mine.shape[1]
    vmem = pl.BlockSpec(memory_space=pltpu.VMEM)
    return pl.pallas_call(
        right_kernel,
        in_specs=[pl.BlockSpec(memory_space=pltpu.SMEM), vmem, vmem, vmem],
        out_specs=(vmem, vmem),
        out_shape=(
            jax.ShapeDtypeStruct((RANK, columns), jnp.float32),
            jax.ShapeDtypeStruct((16, 8, RANK), jnp.float32),
        ),
        compiler_params=params(40),
        cost_estimate=pl.CostEstimate(flops=1300000000, bytes_accessed=3400000, transcendentals=0),
        name="right_part",
    )(core, w, mine, other)


def low_rank(ortho, high_ref, low_ref, start, stop):
    count = ortho.shape[0] // 2
    total = product(ortho, high_ref[:, start:stop])
    return total[:count] + total[count:] + product(ortho[:count], low_ref[:, start:stop])


def momentum_kernel(m_ref, g_ref, ortho_ref, right_ref, out_ref, turned_ref, high_ref, low_ref):
    columns = right_ref.shape[1]

    @pl.when(pl.program_id(0) == 0)
    def _():
        for start in range(0, columns, HALF):
            block = right_ref[:, start : start + HALF]
            high_ref[:, start : start + HALF], low_ref[:, start : start + HALF] = halves(block)
            turned_ref[start : start + HALF, :] = block.T

    ortho = jnp.concatenate(halves(ortho_ref[...]), axis=0)
    for start in range(0, columns, 256):
        stop = min(start + 256, columns)
        buffer = m_ref[:, start:stop].astype(jnp.float32) + g_ref[:, start:stop].astype(jnp.float32)
        update = low_rank(ortho, high_ref, low_ref, start, stop)
        out_ref[:, start:stop] = (buffer - (1.0 - decay) * update).astype(jnp.bfloat16)


def momentum_part(momentum, gradient, ortho, right):
    rows, columns = momentum.shape
    step = rows // 4
    block = pl.BlockSpec((step, columns), lambda i: (i, 0))
    wide = pl.BlockSpec((RANK, columns), lambda i: (0, 0))
    return pl.pallas_call(
        momentum_kernel,
        grid=(4,),
        in_specs=[block, block, pl.BlockSpec((step, RANK), lambda i: (i, 0)), wide],
        out_specs=(block, pl.BlockSpec((columns, RANK), lambda i: (0, 0)), wide, wide),
        out_shape=(
            jax.ShapeDtypeStruct((rows, columns), jnp.bfloat16),
            jax.ShapeDtypeStruct((columns, RANK), jnp.float32),
            jax.ShapeDtypeStruct((RANK, columns), jnp.bfloat16),
            jax.ShapeDtypeStruct((RANK, columns), jnp.bfloat16),
        ),
        compiler_params=params(60),
        cost_estimate=pl.CostEstimate(flops=1308622848, bytes_accessed=7500000, transcendentals=0),
        name="momentum_part",
    )(momentum, gradient, ortho, right)


def weight_kernel(squares_ref, weight_ref, ortho_ref, turned_ref, high_ref, low_ref, out_ref, factor_ref):
    squares = jnp.sum(squares_ref[...], axis=0)[0:1]
    scale = 1.0 / jnp.sqrt(squares / COLS + 1e-06)
    rate = step_size * (ROWS / RANK) ** 0.5
    ortho = jnp.concatenate(halves(ortho_ref[...] * (scale * rate)), axis=0)
    columns = high_ref.shape[1]
    for start in range(0, columns, 256):
        stop = min(start + 256, columns)
        update = low_rank(ortho, high_ref, low_ref, start, stop)
        out_ref[:, start:stop] = (weight_ref[:, start:stop].astype(jnp.float32) - update).astype(
            jnp.bfloat16
        )
    factor_ref[...] = turned_ref[...] * scale


def weight_part(squares, weight, ortho, turned, high, low):
    rows, columns = weight.shape
    step = rows // 4
    block = pl.BlockSpec((step, columns), lambda i: (i, 0))
    wide = pl.BlockSpec((RANK, columns), lambda i: (0, 0))
    factor = pl.BlockSpec((columns // 4, RANK), lambda i: (i, 0))
    return pl.pallas_call(
        weight_kernel,
        grid=(4,),
        in_specs=[
            pl.BlockSpec((16, 8, RANK), lambda i: (0, 0, 0)),
            block,
            pl.BlockSpec((step, RANK), lambda i: (i, 0)),
            factor,
            wide,
            wide,
        ],
        out_specs=(block, factor),
        out_shape=(
            jax.ShapeDtypeStruct((rows, columns), jnp.bfloat16),
            jax.ShapeDtypeStruct((columns, RANK), jnp.float32),
        ),
        compiler_params=params(60),
        cost_estimate=pl.CostEstimate(flops=1308622848, bytes_accessed=7500000, transcendentals=0),
        name="weight_part",
    )(squares, weight, ortho, turned, high, low)


def exchange(pieces, axis, groups=None):
    return lax.all_to_all(pieces, axis, 0, 0, axis_index_groups=groups)


def spread(piece, axis, count, groups=None):
    return exchange(jnp.broadcast_to(piece[None], (count,) + piece.shape), axis, groups)


def swap(value, axis, bits):
    return lax.ppermute(value, axis, [(i, i ^ bits) for i in range(16)])


def z_shift(k):
    return [(z * 2 + c, ((z + k) % 8) * 2 + c) for z in range(8) for c in range(2)]


def gather_near(piece, unit):
    return jnp.concatenate([piece] + [swap(piece, "col", k * unit) for k in (1, 2, 3)], axis=0)


def scatter_z(pieces, gram):
    z = lax.axis_index("row") // 2

    def own(k):
        return lax.dynamic_index_in_dim(pieces, (z + k) % 8, 0, keepdims=False)

    down, up = own(-4), own(3)
    for k, bits in enumerate((2, 4, 14)):
        down = lax.ppermute(down, "row", z_shift(-1)) + own(k - 3)
        up = lax.ppermute(up, "row", z_shift(1))
        up = up + own(2 - k)
        gram = gram + swap(gram, "row", bits)
        down, up, gram = lax.optimization_barrier((down, up, gram))
    gram = gather_near(gram[None], 1)
    total = up + lax.ppermute(down, "row", z_shift(-1))
    return lax.optimization_barrier((total, gram))


def local(gradient, momentum, weight, right_factor):
    core = (lax.axis_index("row") % 2).reshape(1)
    col = lax.axis_index("col")
    partial = left_part(momentum, gradient, right_factor)
    piece = jnp.sum(exchange(partial.reshape(16, 32, RANK), "col"), axis=0)
    left = spread(piece, "col", 16).reshape(512, RANK)
    gram = dot_tn(lax.dynamic_slice(left, (0, col * 16), (512, 16)), left)
    left, gram = lax.optimization_barrier((left, gram))
    gram = gram + swap(gram, "row", 1)
    mine, other = cross_part(core, left, momentum, gradient)
    mine = mine + lax.ppermute(other, "row", CORE_SWAP)
    mine, gram = lax.optimization_barrier((mine, gram))
    mine, gram = scatter_z(mine.reshape(8, 16, 1664), gram)
    gram = gather_near(gram, 4)
    mine = spread(mine, "row", 8, Z_GROUPS).reshape(HALF, 1664)
    jitter, first, gram = first_part(col.reshape(1), gram)
    inverse, ortho = second_part(jitter, first, gram, left)
    mine, inverse = lax.optimization_barrier((mine, inverse))
    other = lax.ppermute(mine, "row", CORE_SWAP)
    right, squares = right_part(core, inverse, mine, other)
    squares = exchange(squares, "col")
    new_momentum, turned, high, low = momentum_part(momentum, gradient, ortho, right)
    new_weight, new_factor = weight_part(squares, weight, ortho, turned, high, low)
    return (new_weight, new_momentum, new_factor)


def solution(mesh):
    in_specs = (P("row", "col"), P("row", "col"), P("row", "col"), P("col", None))
    out_specs = (P("row", "col"), P("row", "col"), P("col", None))
    return jax.shard_map(local, mesh=mesh, in_specs=in_specs, out_specs=out_specs, check_vma=False)
```

```python
import jax
import jax.numpy as jnp
from jax import lax
from jax.experimental import pallas as pl
from jax.experimental.pallas import tpu as pltpu
from jax.sharding import PartitionSpec as P

ROWS = 8192
COLS = 26624
RANK = 256
HIGHEST = lax.Precision.HIGHEST
HIGH = lax.Precision.HIGH

decay = 0.95
step_size = 0.3

HALF = 128
GROUPS = HALF // 8
CORE_SWAP = [(i, i ^ 1) for i in range(16)]
Z_GROUPS = [[z * 2 + c for z in range(8)] for c in range(2)]


def dot_nt(a, b, precision=HIGHEST):
    return lax.dot_general(
        a, b, (((1,), (1,)), ((), ())), precision=precision, preferred_element_type=jnp.float32
    )


def dot_nn(a, b, precision=HIGHEST):
    return lax.dot_general(
        a, b, (((1,), (0,)), ((), ())), precision=precision, preferred_element_type=jnp.float32
    )


def dot_tn(a, b, precision=HIGHEST):
    return lax.dot_general(
        a, b, (((0,), (0,)), ((), ())), precision=precision, preferred_element_type=jnp.float32
    )


def inverse_factor(block):
    rows = lax.broadcasted_iota(jnp.int32, (8, HALF), 0)
    lanes = lax.broadcasted_iota(jnp.int32, (8, HALF), 1)
    a = [block[8 * g : 8 * g + 8, :] for g in range(GROUPS)]
    x = [jnp.where(lanes == rows + 8 * g, 1.0, 0.0).astype(jnp.float32) for g in range(GROUPS)]

    def lane(value, j):
        return jnp.broadcast_to(value[:, j : j + 1], (8, HALF))

    def row(value, s):
        return jnp.broadcast_to(value[s : s + 1, :], (8, HALF))

    done = []
    for g in range(GROUPS):
        columns = [lane(a[g], 8 * g + t) for t in range(8)]
        d = {(s, t): row(columns[t], s) for s in range(8) for t in range(s + 1)}
        a_rows = [row(a[g], t) for t in range(8)]
        x_rows = [row(x[g], t) for t in range(8)]
        inverse = []
        scale = jnp.ones((8, HALF), jnp.float32)
        for k in range(8):
            inverse.append(1.0 / d[k, k])
            scale = jnp.where(rows == k, d[k, k], scale)
            raw = [d.get((s, k)) for s in range(8)]
            for s in range(k + 1, 8):
                ratio = raw[s] * inverse[k]
                for t in range(k + 1, s + 1):
                    d[s, t] = d[s, t] - ratio * raw[t]
                a_rows[s] = a_rows[s] - ratio * a_rows[k]
                x_rows[s] = x_rows[s] - ratio * x_rows[k]
                d[s, k] = ratio
        final = x_rows[0]
        for s in range(1, 8):
            final = jnp.where(rows == s, x_rows[s], final)
        root = lax.rsqrt(scale)
        root = root * (1.5 - 0.5 * scale * root * root)
        done.append(final * root)
        if g == GROUPS - 1:
            break
        for t in range(7, -1, -1):
            a_rows[t] = a_rows[t] * inverse[t]
            x_rows[t] = x_rows[t] * inverse[t]
            for s in range(t + 1, 8):
                a_rows[t] = a_rows[t] - d[s, t] * a_rows[s]
                x_rows[t] = x_rows[t] - d[s, t] * x_rows[s]
        for h in range(g + 1, GROUPS):
            columns = [lane(a[h], 8 * g + t) for t in range(8)]
            for t in range(8):
                a[h] = a[h] - columns[t] * a_rows[t]
                x[h] = x[h] - columns[t] * x_rows[t]
    return jnp.concatenate(done, axis=0)


def first_kernel(col_ref, gather_ref, jitter_ref, w_ref, gram_ref):
    for k in range(16):
        gram_ref[16 * k : 16 * k + 16, :] = gather_ref[col_ref[0] ^ k]
    gram = gram_ref[...]
    eye = lax.broadcasted_iota(jnp.int32, (RANK, RANK), 0) == lax.broadcasted_iota(
        jnp.int32, (RANK, RANK), 1
    )
    jitter = 1e-06 * jnp.sum(jnp.where(eye, gram, 0.0)) / RANK
    jitter_ref[...] = jnp.full((8, HALF), jitter, jnp.float32)
    rows = lax.broadcasted_iota(jnp.int32, (HALF, HALF), 0)
    lanes = lax.broadcasted_iota(jnp.int32, (HALF, HALF), 1)
    w_ref[...] = inverse_factor(gram[:HALF, :HALF] + jnp.where(rows == lanes, jitter, 0.0))


def second_kernel(gram_ref, jitter_ref, first_ref, w_ref):
    first = first_ref[...]
    rows = lax.broadcasted_iota(jnp.int32, (HALF, HALF), 0)
    lanes = lax.broadcasted_iota(jnp.int32, (HALF, HALF), 1)
    low = dot_nt(gram_ref[HALF:, :HALF], first)
    rest = gram_ref[HALF:, HALF:] + jnp.where(rows == lanes, jitter_ref[0:1, :], 0.0)
    second = inverse_factor(rest - dot_nt(low, low))
    w_ref[:HALF, :HALF] = first
    w_ref[:HALF, HALF:] = jnp.zeros((HALF, HALF), jnp.float32)
    w_ref[HALF:, :HALF] = -dot_nn(second, dot_nn(low, first))
    w_ref[HALF:, HALF:] = second


def first_part(col, gather):
    vmem = pl.BlockSpec(memory_space=pltpu.VMEM)
    return pl.pallas_call(
        first_kernel,
        in_specs=[pl.BlockSpec(memory_space=pltpu.SMEM), vmem],
        out_specs=(vmem, vmem, vmem),
        out_shape=(
            jax.ShapeDtypeStruct((8, HALF), jnp.float32),
            jax.ShapeDtypeStruct((HALF, HALF), jnp.float32),
            jax.ShapeDtypeStruct((RANK, RANK), jnp.float32),
        ),
        compiler_params=params(24),
        cost_estimate=pl.CostEstimate(flops=6000000, bytes_accessed=20000000, transcendentals=0),
        name="first_factor",
    )(col, gather)


def second_part(jitter, first, gram):
    return pl.pallas_call(
        second_kernel,
        out_shape=jax.ShapeDtypeStruct((RANK, RANK), jnp.float32),
        compiler_params=params(24),
        cost_estimate=pl.CostEstimate(flops=6000000, bytes_accessed=24000000, transcendentals=0),
        name="second_factor",
    )(gram, jitter, first)


def halves(value):
    high = value.astype(jnp.bfloat16)
    return high, (value - high.astype(jnp.float32)).astype(jnp.bfloat16)


def product(a, b):
    return jnp.dot(a, b, preferred_element_type=jnp.float32)


def params(mib=40):
    return pltpu.CompilerParams(vmem_limit_bytes=mib * 1024 * 1024)


def left_kernel(m_ref, g_ref, r_ref, out_ref, high_ref, low_ref):
    @pl.when(pl.program_id(0) == 0)
    def _():
        high_ref[...], low_ref[...] = halves(r_ref[...])

    both = jnp.concatenate([m_ref[...], g_ref[...]], axis=0)
    total = product(both, high_ref[...]) + product(both, low_ref[...])
    count = m_ref.shape[0]
    out_ref[...] = total[:count] + total[count:]


def left_part(momentum, gradient, right_factor):
    rows, columns = momentum.shape
    step = rows // 2
    block = pl.BlockSpec((step, columns), lambda i: (i, 0))
    return pl.pallas_call(
        left_kernel,
        grid=(2,),
        in_specs=[block, block, pl.BlockSpec((columns, RANK), lambda i: (0, 0))],
        out_specs=pl.BlockSpec((step, RANK), lambda i: (i, 0)),
        out_shape=jax.ShapeDtypeStruct((rows, RANK), jnp.float32),
        scratch_shapes=[pltpu.VMEM((columns, RANK), jnp.bfloat16)] * 2,
        compiler_params=params(60),
        cost_estimate=pl.CostEstimate(flops=1744830464, bytes_accessed=5600000, transcendentals=0),
        name="left_part",
    )(momentum, gradient, right_factor)


def cross_kernel(core_ref, left_ref, m_ref, g_ref, mine_ref, other_ref, lhs_ref):
    turned = left_ref[...].T
    top, bottom = turned[:HALF], turned[HALF:]
    first = core_ref[0] == 0
    own = jnp.where(first, top, bottom)
    far = jnp.where(first, bottom, top)
    lhs_ref[0:HALF], lhs_ref[2 * HALF : 3 * HALF] = halves(own)
    lhs_ref[HALF : 2 * HALF], lhs_ref[3 * HALF :] = halves(far)
    columns = m_ref.shape[1]
    for start in range(0, columns, 256):
        stop = min(start + 256, columns)
        total = product(lhs_ref[...], m_ref[:, start:stop]) + product(lhs_ref[...], g_ref[:, start:stop])
        total = total[: 2 * HALF] + total[2 * HALF :]
        mine_ref[:, start:stop] = total[:HALF]
        other_ref[:, start:stop] = total[HALF:]


def cross_part(core, left, momentum, gradient):
    rows, columns = momentum.shape
    vmem = pl.BlockSpec(memory_space=pltpu.VMEM)
    return pl.pallas_call(
        cross_kernel,
        in_specs=[pl.BlockSpec(memory_space=pltpu.SMEM), vmem, vmem, vmem],
        out_specs=(vmem, vmem),
        out_shape=(jax.ShapeDtypeStruct((HALF, columns), jnp.float32),) * 2,
        scratch_shapes=[pltpu.VMEM((2 * RANK, rows), jnp.bfloat16)],
        compiler_params=params(),
        cost_estimate=pl.CostEstimate(flops=1744830464, bytes_accessed=5600000, transcendentals=0),
        name="cross_part",
    )(core, left, momentum, gradient)


def right_kernel(core_ref, w_ref, mine_ref, other_ref, right_ref, squares_ref):
    w = w_ref[...]
    whole = jnp.zeros((RANK, HALF), jnp.float32)
    first = core_ref[0] == 0
    columns = mine_ref.shape[1]
    for start in range(0, columns, 256):
        stop = min(start + 256, columns)
        mine, other = mine_ref[:, start:stop], other_ref[:, start:stop]
        y = jnp.concatenate([jnp.where(first, mine, other), jnp.where(first, other, mine)], axis=0)
        right = dot_nn(w, y)
        right_ref[:, start:stop] = right
        square = right * right
        for k in range(0, stop - start, HALF):
            whole = whole + square[:, k : k + HALF]
    total = jnp.sum(whole.T, axis=0, keepdims=True)
    squares_ref[...] = jnp.broadcast_to(total[None], squares_ref.shape)


def right_part(core, w, mine, other):
    columns = mine.shape[1]
    vmem = pl.BlockSpec(memory_space=pltpu.VMEM)
    return pl.pallas_call(
        right_kernel,
        in_specs=[pl.BlockSpec(memory_space=pltpu.SMEM), vmem, vmem, vmem],
        out_specs=(vmem, vmem),
        out_shape=(
            jax.ShapeDtypeStruct((RANK, columns), jnp.float32),
            jax.ShapeDtypeStruct((16, 8, RANK), jnp.float32),
        ),
        compiler_params=params(40),
        cost_estimate=pl.CostEstimate(flops=1300000000, bytes_accessed=3400000, transcendentals=0),
        name="right_part",
    )(core, w, mine, other)


def low_rank(ortho, high_ref, low_ref, start, stop):
    count = ortho.shape[0] // 2
    total = product(ortho, high_ref[:, start:stop])
    return total[:count] + total[count:] + product(ortho[:count], low_ref[:, start:stop])


def momentum_kernel(
    m_ref, g_ref, left_ref, w_ref, right_ref, out_ref, turned_ref, high_ref, low_ref, ortho_ref
):
    columns = right_ref.shape[1]

    @pl.when(pl.program_id(0) == 0)
    def _():
        for start in range(0, columns, HALF):
            block = right_ref[:, start : start + HALF]
            high_ref[:, start : start + HALF], low_ref[:, start : start + HALF] = halves(block)
            turned_ref[start : start + HALF, :] = block.T

    ortho = dot_nt(left_ref[...], w_ref[...])
    ortho_ref[...] = ortho
    ortho = jnp.concatenate(halves(ortho), axis=0)
    for start in range(0, columns, 256):
        stop = min(start + 256, columns)
        buffer = m_ref[:, start:stop].astype(jnp.float32) + g_ref[:, start:stop].astype(jnp.float32)
        update = low_rank(ortho, high_ref, low_ref, start, stop)
        out_ref[:, start:stop] = (buffer - (1.0 - decay) * update).astype(jnp.bfloat16)


def momentum_part(momentum, gradient, left, w, right):
    rows, columns = momentum.shape
    step = rows // 4
    block = pl.BlockSpec((step, columns), lambda i: (i, 0))
    thin = pl.BlockSpec((step, RANK), lambda i: (i, 0))
    wide = pl.BlockSpec((RANK, columns), lambda i: (0, 0))
    return pl.pallas_call(
        momentum_kernel,
        grid=(4,),
        in_specs=[block, block, thin, pl.BlockSpec((RANK, RANK), lambda i: (0, 0)), wide],
        out_specs=(block, pl.BlockSpec((columns, RANK), lambda i: (0, 0)), wide, wide, thin),
        out_shape=(
            jax.ShapeDtypeStruct((rows, columns), jnp.bfloat16),
            jax.ShapeDtypeStruct((columns, RANK), jnp.float32),
            jax.ShapeDtypeStruct((RANK, columns), jnp.bfloat16),
            jax.ShapeDtypeStruct((RANK, columns), jnp.bfloat16),
            jax.ShapeDtypeStruct((rows, RANK), jnp.float32),
        ),
        compiler_params=params(60),
        cost_estimate=pl.CostEstimate(flops=1308622848, bytes_accessed=7500000, transcendentals=0),
        name="momentum_part",
    )(momentum, gradient, left, w, right)


def weight_kernel(squares_ref, weight_ref, ortho_ref, turned_ref, high_ref, low_ref, out_ref, factor_ref):
    squares = jnp.sum(squares_ref[...], axis=0)[0:1]
    scale = 1.0 / jnp.sqrt(squares / COLS + 1e-06)
    rate = step_size * (ROWS / RANK) ** 0.5
    ortho = jnp.concatenate(halves(ortho_ref[...] * (scale * rate)), axis=0)
    columns = high_ref.shape[1]
    for start in range(0, columns, 256):
        stop = min(start + 256, columns)
        update = low_rank(ortho, high_ref, low_ref, start, stop)
        out_ref[:, start:stop] = (weight_ref[:, start:stop].astype(jnp.float32) - update).astype(
            jnp.bfloat16
        )
    factor_ref[...] = turned_ref[...] * scale


def weight_part(squares, weight, ortho, turned, high, low):
    rows, columns = weight.shape
    step = rows // 2
    block = pl.BlockSpec((step, columns), lambda i: (i, 0))
    wide = pl.BlockSpec((RANK, columns), lambda i: (0, 0))
    factor = pl.BlockSpec((columns // 2, RANK), lambda i: (i, 0))
    return pl.pallas_call(
        weight_kernel,
        grid=(2,),
        in_specs=[
            pl.BlockSpec((16, 8, RANK), lambda i: (0, 0, 0)),
            block,
            pl.BlockSpec((step, RANK), lambda i: (i, 0)),
            factor,
            wide,
            wide,
        ],
        out_specs=(block, factor),
        out_shape=(
            jax.ShapeDtypeStruct((rows, columns), jnp.bfloat16),
            jax.ShapeDtypeStruct((columns, RANK), jnp.float32),
        ),
        compiler_params=params(60),
        cost_estimate=pl.CostEstimate(flops=1308622848, bytes_accessed=7500000, transcendentals=0),
        name="weight_part",
    )(squares, weight, ortho, turned, high, low)


def exchange(pieces, axis, groups=None):
    return lax.all_to_all(pieces, axis, 0, 0, axis_index_groups=groups)


def spread(piece, axis, count, groups=None):
    return exchange(jnp.broadcast_to(piece[None], (count,) + piece.shape), axis, groups)


def swap(value, axis, bits):
    return lax.ppermute(value, axis, [(i, i ^ bits) for i in range(16)])


def z_shift(k):
    return [(z * 2 + c, ((z + k) % 8) * 2 + c) for z in range(8) for c in range(2)]


def gather_near(piece, unit):
    return jnp.concatenate([piece] + [swap(piece, "col", k * unit) for k in (1, 2, 3)], axis=0)


def scatter_z(pieces, gram):
    z = lax.axis_index("row") // 2

    def own(k):
        return lax.dynamic_index_in_dim(pieces, (z + k) % 8, 0, keepdims=False)

    down, up = own(-4), own(3)
    for k, bits in enumerate((2, 4, 14)):
        down = lax.ppermute(down, "row", z_shift(-1)) + own(k - 3)
        up = lax.ppermute(up, "row", z_shift(1))
        up = up + own(2 - k)
        gram = gram + swap(gram, "row", bits)
        down, up, gram = lax.optimization_barrier((down, up, gram))
    gram = gather_near(gram[None], 1)
    total = up + lax.ppermute(down, "row", z_shift(-1))
    return lax.optimization_barrier((total, gram))


def local(gradient, momentum, weight, right_factor):
    core = (lax.axis_index("row") % 2).reshape(1)
    col = lax.axis_index("col")
    partial = left_part(momentum, gradient, right_factor)
    piece = jnp.sum(exchange(partial.reshape(16, 32, RANK), "col"), axis=0)
    left = spread(piece, "col", 16).reshape(512, RANK)
    gram = dot_tn(lax.dynamic_slice(left, (0, col * 16), (512, 16)), left)
    left, gram = lax.optimization_barrier((left, gram))
    gram = gram + swap(gram, "row", 1)
    mine, other = cross_part(core, left, momentum, gradient)
    mine = mine + lax.ppermute(other, "row", CORE_SWAP)
    mine, gram = lax.optimization_barrier((mine, gram))
    mine, gram = scatter_z(mine.reshape(8, 16, 1664), gram)
    gram = gather_near(gram, 4)
    mine = spread(mine, "row", 8, Z_GROUPS).reshape(HALF, 1664)
    jitter, first, gram = first_part(col.reshape(1), gram)
    inverse = second_part(jitter, first, gram)
    mine, inverse = lax.optimization_barrier((mine, inverse))
    other = lax.ppermute(mine, "row", CORE_SWAP)
    right, squares = right_part(core, inverse, mine, other)
    squares = exchange(squares, "col")
    new_momentum, turned, high, low, ortho = momentum_part(
        momentum, gradient, left, inverse, right
    )
    new_weight, new_factor = weight_part(squares, weight, ortho, turned, high, low)
    return (new_weight, new_momentum, new_factor)


def solution(mesh):
    in_specs = (P("row", "col"), P("row", "col"), P("row", "col"), P("col", None))
    out_specs = (P("row", "col"), P("row", "col"), P("col", None))
    return jax.shard_map(local, mesh=mesh, in_specs=in_specs, out_specs=out_specs, check_vma=False)
```

```python
import jax
import jax.numpy as jnp
from jax import lax
from jax.experimental import pallas as pl
from jax.experimental.pallas import tpu as pltpu
from jax.sharding import PartitionSpec as P

ROWS = 8192
COLS = 26624
RANK = 256
HIGHEST = lax.Precision.HIGHEST
HIGH = lax.Precision.HIGH

decay = 0.95
step_size = 0.3

HALF = 128
GROUPS = HALF // 8
CORE_SWAP = [(i, i ^ 1) for i in range(16)]
Z_GROUPS = [[z * 2 + c for z in range(8)] for c in range(2)]


def dot_nt(a, b, precision=HIGHEST):
    return lax.dot_general(
        a, b, (((1,), (1,)), ((), ())), precision=precision, preferred_element_type=jnp.float32
    )


def dot_nn(a, b, precision=HIGHEST):
    return lax.dot_general(
        a, b, (((1,), (0,)), ((), ())), precision=precision, preferred_element_type=jnp.float32
    )


def dot_tn(a, b, precision=HIGHEST):
    return lax.dot_general(
        a, b, (((0,), (0,)), ((), ())), precision=precision, preferred_element_type=jnp.float32
    )


def inverse_factor(block):
    rows = lax.broadcasted_iota(jnp.int32, (8, HALF), 0)
    lanes = lax.broadcasted_iota(jnp.int32, (8, HALF), 1)
    a = [block[8 * g : 8 * g + 8, :] for g in range(GROUPS)]
    x = [jnp.where(lanes == rows + 8 * g, 1.0, 0.0).astype(jnp.float32) for g in range(GROUPS)]

    def lane(value, j):
        return jnp.broadcast_to(value[:, j : j + 1], (8, HALF))

    def row(value, s):
        return jnp.broadcast_to(value[s : s + 1, :], (8, HALF))

    done = []
    for g in range(GROUPS):
        columns = [lane(a[g], 8 * g + t) for t in range(8)]
        d = {(s, t): row(columns[t], s) for s in range(8) for t in range(s + 1)}
        a_rows = [row(a[g], t) for t in range(8)]
        x_rows = [row(x[g], t) for t in range(8)]
        inverse = []
        scale = jnp.ones((8, HALF), jnp.float32)
        for k in range(8):
            inverse.append(1.0 / d[k, k])
            scale = jnp.where(rows == k, d[k, k], scale)
            raw = [d.get((s, k)) for s in range(8)]
            for s in range(k + 1, 8):
                ratio = raw[s] * inverse[k]
                for t in range(k + 1, s + 1):
                    d[s, t] = d[s, t] - ratio * raw[t]
                a_rows[s] = a_rows[s] - ratio * a_rows[k]
                x_rows[s] = x_rows[s] - ratio * x_rows[k]
                d[s, k] = ratio
        final = x_rows[0]
        for s in range(1, 8):
            final = jnp.where(rows == s, x_rows[s], final)
        root = lax.rsqrt(scale)
        root = root * (1.5 - 0.5 * scale * root * root)
        done.append(final * root)
        if g == GROUPS - 1:
            break
        for t in range(7, -1, -1):
            a_rows[t] = a_rows[t] * inverse[t]
            x_rows[t] = x_rows[t] * inverse[t]
            for s in range(t + 1, 8):
                a_rows[t] = a_rows[t] - d[s, t] * a_rows[s]
                x_rows[t] = x_rows[t] - d[s, t] * x_rows[s]
        for h in range(g + 1, GROUPS):
            columns = [lane(a[h], 8 * g + t) for t in range(8)]
            for t in range(8):
                a[h] = a[h] - columns[t] * a_rows[t]
                x[h] = x[h] - columns[t] * x_rows[t]
    return jnp.concatenate(done, axis=0)


def first_kernel(col_ref, gather_ref, jitter_ref, w_ref, gram_ref):
    for k in range(16):
        gram_ref[16 * k : 16 * k + 16, :] = gather_ref[col_ref[0] ^ k]
    gram = gram_ref[...]
    eye = lax.broadcasted_iota(jnp.int32, (RANK, RANK), 0) == lax.broadcasted_iota(
        jnp.int32, (RANK, RANK), 1
    )
    jitter = 1e-06 * jnp.sum(jnp.where(eye, gram, 0.0)) / RANK
    jitter_ref[...] = jnp.full((8, HALF), jitter, jnp.float32)
    rows = lax.broadcasted_iota(jnp.int32, (HALF, HALF), 0)
    lanes = lax.broadcasted_iota(jnp.int32, (HALF, HALF), 1)
    w_ref[...] = inverse_factor(gram[:HALF, :HALF] + jnp.where(rows == lanes, jitter, 0.0))


def second_kernel(gram_ref, jitter_ref, first_ref, w_ref):
    first = first_ref[...]
    rows = lax.broadcasted_iota(jnp.int32, (HALF, HALF), 0)
    lanes = lax.broadcasted_iota(jnp.int32, (HALF, HALF), 1)
    low = dot_nt(gram_ref[HALF:, :HALF], first)
    rest = gram_ref[HALF:, HALF:] + jnp.where(rows == lanes, jitter_ref[0:1, :], 0.0)
    second = inverse_factor(rest - dot_nt(low, low))
    w_ref[:HALF, :HALF] = first
    w_ref[:HALF, HALF:] = jnp.zeros((HALF, HALF), jnp.float32)
    w_ref[HALF:, :HALF] = -dot_nn(second, dot_nn(low, first))
    w_ref[HALF:, HALF:] = second


def first_part(col, gather):
    vmem = pl.BlockSpec(memory_space=pltpu.VMEM)
    return pl.pallas_call(
        first_kernel,
        in_specs=[pl.BlockSpec(memory_space=pltpu.SMEM), vmem],
        out_specs=(vmem, vmem, vmem),
        out_shape=(
            jax.ShapeDtypeStruct((8, HALF), jnp.float32),
            jax.ShapeDtypeStruct((HALF, HALF), jnp.float32),
            jax.ShapeDtypeStruct((RANK, RANK), jnp.float32),
        ),
        compiler_params=params(24),
        cost_estimate=pl.CostEstimate(flops=6000000, bytes_accessed=20000000, transcendentals=0),
        name="first_factor",
    )(col, gather)


def second_part(jitter, first, gram):
    return pl.pallas_call(
        second_kernel,
        out_shape=jax.ShapeDtypeStruct((RANK, RANK), jnp.float32),
        compiler_params=params(24),
        cost_estimate=pl.CostEstimate(flops=6000000, bytes_accessed=24000000, transcendentals=0),
        name="second_factor",
    )(gram, jitter, first)


def halves(value):
    high = value.astype(jnp.bfloat16)
    return high, (value - high.astype(jnp.float32)).astype(jnp.bfloat16)


def product(a, b):
    return jnp.dot(a, b, preferred_element_type=jnp.float32)


def params(mib=40):
    return pltpu.CompilerParams(vmem_limit_bytes=mib * 1024 * 1024)


def left_kernel(m_ref, g_ref, r_ref, out_ref, high_ref, low_ref):
    @pl.when(pl.program_id(0) == 0)
    def _():
        high_ref[...], low_ref[...] = halves(r_ref[...])

    both = jnp.concatenate([m_ref[...], g_ref[...]], axis=0)
    total = product(both, high_ref[...]) + product(both, low_ref[...])
    count = m_ref.shape[0]
    out_ref[...] = total[:count] + total[count:]


def left_part(momentum, gradient, right_factor):
    rows, columns = momentum.shape
    step = rows // 2
    block = pl.BlockSpec((step, columns), lambda i: (i, 0))
    return pl.pallas_call(
        left_kernel,
        grid=(2,),
        in_specs=[block, block, pl.BlockSpec((columns, RANK), lambda i: (0, 0))],
        out_specs=pl.BlockSpec((step, RANK), lambda i: (i, 0)),
        out_shape=jax.ShapeDtypeStruct((rows, RANK), jnp.float32),
        scratch_shapes=[pltpu.VMEM((columns, RANK), jnp.bfloat16)] * 2,
        compiler_params=params(60),
        cost_estimate=pl.CostEstimate(flops=1744830464, bytes_accessed=5600000, transcendentals=0),
        name="left_part",
    )(momentum, gradient, right_factor)


def cross_kernel(core_ref, left_ref, m_ref, g_ref, mine_ref, other_ref, lhs_ref):
    turned = left_ref[...].T
    top, bottom = turned[:HALF], turned[HALF:]
    first = core_ref[0] == 0
    own = jnp.where(first, top, bottom)
    far = jnp.where(first, bottom, top)
    lhs_ref[0:HALF], lhs_ref[2 * HALF : 3 * HALF] = halves(own)
    lhs_ref[HALF : 2 * HALF], lhs_ref[3 * HALF :] = halves(far)
    columns = m_ref.shape[1]
    for start in range(0, columns, 256):
        stop = min(start + 256, columns)
        total = product(lhs_ref[...], m_ref[:, start:stop]) + product(lhs_ref[...], g_ref[:, start:stop])
        total = total[: 2 * HALF] + total[2 * HALF :]
        mine_ref[:, start:stop] = total[:HALF]
        other_ref[:, start:stop] = total[HALF:]


def cross_part(core, left, momentum, gradient):
    rows, columns = momentum.shape
    vmem = pl.BlockSpec(memory_space=pltpu.VMEM)
    return pl.pallas_call(
        cross_kernel,
        in_specs=[pl.BlockSpec(memory_space=pltpu.SMEM), vmem, vmem, vmem],
        out_specs=(vmem, vmem),
        out_shape=(jax.ShapeDtypeStruct((HALF, columns), jnp.float32),) * 2,
        scratch_shapes=[pltpu.VMEM((2 * RANK, rows), jnp.bfloat16)],
        compiler_params=params(),
        cost_estimate=pl.CostEstimate(flops=1744830464, bytes_accessed=5600000, transcendentals=0),
        name="cross_part",
    )(core, left, momentum, gradient)


def right_kernel(core_ref, w_ref, mine_ref, other_ref, right_ref, squares_ref):
    w = w_ref[...]
    whole = jnp.zeros((RANK, HALF), jnp.float32)
    first = core_ref[0] == 0
    columns = mine_ref.shape[1]
    for start in range(0, columns, 256):
        stop = min(start + 256, columns)
        mine, other = mine_ref[:, start:stop], other_ref[:, start:stop]
        y = jnp.concatenate([jnp.where(first, mine, other), jnp.where(first, other, mine)], axis=0)
        right = dot_nn(w, y)
        right_ref[:, start:stop] = right
        square = right * right
        for k in range(0, stop - start, HALF):
            whole = whole + square[:, k : k + HALF]
    total = jnp.sum(whole.T, axis=0, keepdims=True)
    squares_ref[...] = jnp.broadcast_to(total[None], squares_ref.shape)


def right_part(core, w, mine, other):
    columns = mine.shape[1]
    vmem = pl.BlockSpec(memory_space=pltpu.VMEM)
    return pl.pallas_call(
        right_kernel,
        in_specs=[pl.BlockSpec(memory_space=pltpu.SMEM), vmem, vmem, vmem],
        out_specs=(vmem, vmem),
        out_shape=(
            jax.ShapeDtypeStruct((RANK, columns), jnp.float32),
            jax.ShapeDtypeStruct((16, 8, RANK), jnp.float32),
        ),
        compiler_params=params(40),
        cost_estimate=pl.CostEstimate(flops=1300000000, bytes_accessed=3400000, transcendentals=0),
        name="right_part",
    )(core, w, mine, other)


def low_rank(ortho, high_ref, low_ref, start, stop):
    count = ortho.shape[0] // 2
    total = product(ortho, high_ref[:, start:stop])
    return total[:count] + total[count:] + product(ortho[:count], low_ref[:, start:stop])


def momentum_kernel(
    m_ref, g_ref, left_ref, w_ref, right_ref, out_ref, turned_ref, high_ref, low_ref, ortho_ref
):
    columns = right_ref.shape[1]

    @pl.when(pl.program_id(0) == 0)
    def _():
        for start in range(0, columns, HALF):
            block = right_ref[:, start : start + HALF]
            high_ref[:, start : start + HALF], low_ref[:, start : start + HALF] = halves(block)
            turned_ref[start : start + HALF, :] = block.T

    ortho = dot_nt(left_ref[...], w_ref[...])
    ortho_ref[...] = ortho
    ortho = jnp.concatenate(halves(ortho), axis=0)
    for start in range(0, columns, 256):
        stop = min(start + 256, columns)
        buffer = m_ref[:, start:stop].astype(jnp.float32) + g_ref[:, start:stop].astype(jnp.float32)
        update = low_rank(ortho, high_ref, low_ref, start, stop)
        out_ref[:, start:stop] = (buffer - (1.0 - decay) * update).astype(jnp.bfloat16)


def momentum_part(momentum, gradient, left, w, right):
    rows, columns = momentum.shape
    step = rows // 2
    block = pl.BlockSpec((step, columns), lambda i: (i, 0))
    thin = pl.BlockSpec((step, RANK), lambda i: (i, 0))
    wide = pl.BlockSpec((RANK, columns), lambda i: (0, 0))
    return pl.pallas_call(
        momentum_kernel,
        grid=(2,),
        in_specs=[block, block, thin, pl.BlockSpec((RANK, RANK), lambda i: (0, 0)), wide],
        out_specs=(block, pl.BlockSpec((columns, RANK), lambda i: (0, 0)), wide, wide, thin),
        out_shape=(
            jax.ShapeDtypeStruct((rows, columns), jnp.bfloat16),
            jax.ShapeDtypeStruct((columns, RANK), jnp.float32),
            jax.ShapeDtypeStruct((RANK, columns), jnp.bfloat16),
            jax.ShapeDtypeStruct((RANK, columns), jnp.bfloat16),
            jax.ShapeDtypeStruct((rows, RANK), jnp.float32),
        ),
        compiler_params=params(60),
        cost_estimate=pl.CostEstimate(flops=1308622848, bytes_accessed=7500000, transcendentals=0),
        name="momentum_part",
    )(momentum, gradient, left, w, right)


def weight_kernel(squares_ref, weight_ref, ortho_ref, turned_ref, high_ref, low_ref, out_ref, factor_ref):
    squares = jnp.sum(squares_ref[...], axis=0)[0:1]
    scale = 1.0 / jnp.sqrt(squares / COLS + 1e-06)
    rate = step_size * (ROWS / RANK) ** 0.5
    ortho = jnp.concatenate(halves(ortho_ref[...] * (scale * rate)), axis=0)
    columns = high_ref.shape[1]
    for start in range(0, columns, 256):
        stop = min(start + 256, columns)
        update = low_rank(ortho, high_ref, low_ref, start, stop)
        out_ref[:, start:stop] = (weight_ref[:, start:stop].astype(jnp.float32) - update).astype(
            jnp.bfloat16
        )
    factor_ref[...] = turned_ref[...] * scale


def weight_part(squares, weight, ortho, turned, high, low):
    rows, columns = weight.shape
    step = rows // 2
    block = pl.BlockSpec((step, columns), lambda i: (i, 0))
    wide = pl.BlockSpec((RANK, columns), lambda i: (0, 0))
    factor = pl.BlockSpec((columns // 2, RANK), lambda i: (i, 0))
    return pl.pallas_call(
        weight_kernel,
        grid=(2,),
        in_specs=[
            pl.BlockSpec((16, 8, RANK), lambda i: (0, 0, 0)),
            block,
            pl.BlockSpec((step, RANK), lambda i: (i, 0)),
            factor,
            wide,
            wide,
        ],
        out_specs=(block, factor),
        out_shape=(
            jax.ShapeDtypeStruct((rows, columns), jnp.bfloat16),
            jax.ShapeDtypeStruct((columns, RANK), jnp.float32),
        ),
        compiler_params=params(60),
        cost_estimate=pl.CostEstimate(flops=1308622848, bytes_accessed=7500000, transcendentals=0),
        name="weight_part",
    )(squares, weight, ortho, turned, high, low)


def exchange(pieces, axis, groups=None):
    return lax.all_to_all(pieces, axis, 0, 0, axis_index_groups=groups)


def spread(piece, axis, count, groups=None):
    return exchange(jnp.broadcast_to(piece[None], (count,) + piece.shape), axis, groups)


def swap(value, axis, bits):
    return lax.ppermute(value, axis, [(i, i ^ bits) for i in range(16)])


def z_shift(k):
    return [(z * 2 + c, ((z + k) % 8) * 2 + c) for z in range(8) for c in range(2)]


def gather_near(piece, unit):
    return jnp.concatenate([piece] + [swap(piece, "col", k * unit) for k in (1, 2, 3)], axis=0)


def scatter_z(pieces, gram):
    z = lax.axis_index("row") // 2

    def own(k):
        return lax.dynamic_index_in_dim(pieces, (z + k) % 8, 0, keepdims=False)

    down, up = own(-4), own(3)
    for k, bits in enumerate((2, 4, 14)):
        down = lax.ppermute(down, "row", z_shift(-1)) + own(k - 3)
        up = lax.ppermute(up, "row", z_shift(1))
        up = up + own(2 - k)
        gram = gram + swap(gram, "row", bits)
        down, up, gram = lax.optimization_barrier((down, up, gram))
    gram = gather_near(gram[None], 1)
    total = up + lax.ppermute(down, "row", z_shift(-1))
    return lax.optimization_barrier((total, gram))


def local(gradient, momentum, weight, right_factor):
    core = (lax.axis_index("row") % 2).reshape(1)
    col = lax.axis_index("col")
    partial = left_part(momentum, gradient, right_factor)
    piece = jnp.sum(exchange(partial.reshape(16, 32, RANK), "col"), axis=0)
    left = spread(piece, "col", 16).reshape(512, RANK)
    gram = dot_tn(lax.dynamic_slice(left, (0, col * 16), (512, 16)), left)
    left, gram = lax.optimization_barrier((left, gram))
    gram = gram + swap(gram, "row", 1)
    mine, other = cross_part(core, left, momentum, gradient)
    mine = mine + lax.ppermute(other, "row", CORE_SWAP)
    mine, gram = lax.optimization_barrier((mine, gram))
    mine, gram = scatter_z(mine.reshape(8, 16, 1664), gram)
    gram = gather_near(gram, 4)
    mine = spread(mine, "row", 8, Z_GROUPS).reshape(HALF, 1664)
    jitter, first, gram = first_part(col.reshape(1), gram)
    inverse = second_part(jitter, first, gram)
    mine, inverse = lax.optimization_barrier((mine, inverse))
    other = lax.ppermute(mine, "row", CORE_SWAP)
    right, squares = right_part(core, inverse, mine, other)
    squares = exchange(squares, "col")
    new_momentum, turned, high, low, ortho = momentum_part(
        momentum, gradient, left, inverse, right
    )
    new_weight, new_factor = weight_part(squares, weight, ortho, turned, high, low)
    return (new_weight, new_momentum, new_factor)


def solution(mesh):
    in_specs = (P("row", "col"), P("row", "col"), P("row", "col"), P("col", None))
    out_specs = (P("row", "col"), P("row", "col"), P("col", None))
    return jax.shard_map(local, mesh=mesh, in_specs=in_specs, out_specs=out_specs, check_vma=False)
```

```python
import jax
import jax.numpy as jnp
from jax import lax
from jax.experimental import pallas as pl
from jax.experimental.pallas import tpu as pltpu
from jax.sharding import PartitionSpec as P

ROWS = 8192
COLS = 26624
RANK = 256
HIGHEST = lax.Precision.HIGHEST
HIGH = lax.Precision.HIGH

decay = 0.95
step_size = 0.3

HALF = 128
GROUPS = HALF // 8
CORE_SWAP = [(i, i ^ 1) for i in range(16)]
Z_GROUPS = [[z * 2 + c for z in range(8)] for c in range(2)]


def dot_nt(a, b, precision=HIGHEST):
    return lax.dot_general(
        a, b, (((1,), (1,)), ((), ())), precision=precision, preferred_element_type=jnp.float32
    )


def dot_nn(a, b, precision=HIGHEST):
    return lax.dot_general(
        a, b, (((1,), (0,)), ((), ())), precision=precision, preferred_element_type=jnp.float32
    )


def dot_tn(a, b, precision=HIGHEST):
    return lax.dot_general(
        a, b, (((0,), (0,)), ((), ())), precision=precision, preferred_element_type=jnp.float32
    )


def inverse_factor(block):
    rows = lax.broadcasted_iota(jnp.int32, (8, HALF), 0)
    lanes = lax.broadcasted_iota(jnp.int32, (8, HALF), 1)
    a = [block[8 * g : 8 * g + 8, :] for g in range(GROUPS)]
    x = [jnp.where(lanes == rows + 8 * g, 1.0, 0.0).astype(jnp.float32) for g in range(GROUPS)]

    def lane(value, j):
        return jnp.broadcast_to(value[:, j : j + 1], (8, HALF))

    def row(value, s):
        return jnp.broadcast_to(value[s : s + 1, :], (8, HALF))

    done = []
    for g in range(GROUPS):
        columns = [lane(a[g], 8 * g + t) for t in range(8)]
        d = {(s, t): row(columns[t], s) for s in range(8) for t in range(s + 1)}
        a_rows = [row(a[g], t) for t in range(8)]
        x_rows = [row(x[g], t) for t in range(8)]
        inverse = []
        scale = jnp.ones((8, HALF), jnp.float32)
        for k in range(8):
            inverse.append(1.0 / d[k, k])
            scale = jnp.where(rows == k, d[k, k], scale)
            raw = [d.get((s, k)) for s in range(8)]
            for s in range(k + 1, 8):
                ratio = raw[s] * inverse[k]
                for t in range(k + 1, s + 1):
                    d[s, t] = d[s, t] - ratio * raw[t]
                a_rows[s] = a_rows[s] - ratio * a_rows[k]
                x_rows[s] = x_rows[s] - ratio * x_rows[k]
                d[s, k] = ratio
        final = x_rows[0]
        for s in range(1, 8):
            final = jnp.where(rows == s, x_rows[s], final)
        root = lax.rsqrt(scale)
        root = root * (1.5 - 0.5 * scale * root * root)
        done.append(final * root)
        if g == GROUPS - 1:
            break
        for t in range(7, -1, -1):
            a_rows[t] = a_rows[t] * inverse[t]
            x_rows[t] = x_rows[t] * inverse[t]
            for s in range(t + 1, 8):
                a_rows[t] = a_rows[t] - d[s, t] * a_rows[s]
                x_rows[t] = x_rows[t] - d[s, t] * x_rows[s]
        for h in range(g + 1, GROUPS):
            columns = [lane(a[h], 8 * g + t) for t in range(8)]
            for t in range(8):
                a[h] = a[h] - columns[t] * a_rows[t]
                x[h] = x[h] - columns[t] * x_rows[t]
    return jnp.concatenate(done, axis=0)


def first_kernel(col_ref, gather_ref, jitter_ref, w_ref, gram_ref):
    for k in range(16):
        gram_ref[16 * k : 16 * k + 16, :] = gather_ref[col_ref[0] ^ k]
    gram = gram_ref[...]
    eye = lax.broadcasted_iota(jnp.int32, (RANK, RANK), 0) == lax.broadcasted_iota(
        jnp.int32, (RANK, RANK), 1
    )
    jitter = 1e-06 * jnp.sum(jnp.where(eye, gram, 0.0)) / RANK
    jitter_ref[...] = jnp.full((8, HALF), jitter, jnp.float32)
    rows = lax.broadcasted_iota(jnp.int32, (HALF, HALF), 0)
    lanes = lax.broadcasted_iota(jnp.int32, (HALF, HALF), 1)
    w_ref[...] = inverse_factor(gram[:HALF, :HALF] + jnp.where(rows == lanes, jitter, 0.0))


def second_kernel(gram_ref, jitter_ref, first_ref, w_ref):
    first = first_ref[...]
    rows = lax.broadcasted_iota(jnp.int32, (HALF, HALF), 0)
    lanes = lax.broadcasted_iota(jnp.int32, (HALF, HALF), 1)
    low = dot_nt(gram_ref[HALF:, :HALF], first)
    rest = gram_ref[HALF:, HALF:] + jnp.where(rows == lanes, jitter_ref[0:1, :], 0.0)
    second = inverse_factor(rest - dot_nt(low, low))
    w_ref[:HALF, :HALF] = first
    w_ref[:HALF, HALF:] = jnp.zeros((HALF, HALF), jnp.float32)
    w_ref[HALF:, :HALF] = -dot_nn(second, dot_nn(low, first))
    w_ref[HALF:, HALF:] = second


def first_part(col, gather):
    vmem = pl.BlockSpec(memory_space=pltpu.VMEM)
    return pl.pallas_call(
        first_kernel,
        in_specs=[pl.BlockSpec(memory_space=pltpu.SMEM), vmem],
        out_specs=(vmem, vmem, vmem),
        out_shape=(
            jax.ShapeDtypeStruct((8, HALF), jnp.float32),
            jax.ShapeDtypeStruct((HALF, HALF), jnp.float32),
            jax.ShapeDtypeStruct((RANK, RANK), jnp.float32),
        ),
        compiler_params=params(24),
        cost_estimate=pl.CostEstimate(flops=6000000, bytes_accessed=20000000, transcendentals=0),
        name="first_factor",
    )(col, gather)


def second_part(jitter, first, gram):
    return pl.pallas_call(
        second_kernel,
        out_shape=jax.ShapeDtypeStruct((RANK, RANK), jnp.float32),
        compiler_params=params(24),
        cost_estimate=pl.CostEstimate(flops=6000000, bytes_accessed=24000000, transcendentals=0),
        name="second_factor",
    )(gram, jitter, first)


def halves(value):
    high = value.astype(jnp.bfloat16)
    return high, (value - high.astype(jnp.float32)).astype(jnp.bfloat16)


def product(a, b):
    return jnp.dot(a, b, preferred_element_type=jnp.float32)


def params(mib=40):
    return pltpu.CompilerParams(vmem_limit_bytes=mib * 1024 * 1024)


def left_kernel(m_ref, g_ref, r_ref, out_ref, high_ref, low_ref):
    @pl.when(pl.program_id(0) == 0)
    def _():
        high_ref[...], low_ref[...] = halves(r_ref[...])

    both = jnp.concatenate([m_ref[...], g_ref[...]], axis=0)
    total = product(both, high_ref[...]) + product(both, low_ref[...])
    count = m_ref.shape[0]
    out_ref[...] = total[:count] + total[count:]


def left_part(momentum, gradient, right_factor):
    rows, columns = momentum.shape
    step = rows // 2
    block = pl.BlockSpec((step, columns), lambda i: (i, 0))
    return pl.pallas_call(
        left_kernel,
        grid=(2,),
        in_specs=[block, block, pl.BlockSpec((columns, RANK), lambda i: (0, 0))],
        out_specs=pl.BlockSpec((step, RANK), lambda i: (i, 0)),
        out_shape=jax.ShapeDtypeStruct((rows, RANK), jnp.float32),
        scratch_shapes=[pltpu.VMEM((columns, RANK), jnp.bfloat16)] * 2,
        compiler_params=params(60),
        cost_estimate=pl.CostEstimate(flops=1744830464, bytes_accessed=5600000, transcendentals=0),
        name="left_part",
    )(momentum, gradient, right_factor)


def cross_kernel(core_ref, left_ref, m_ref, g_ref, mine_ref, other_ref, lhs_ref):
    turned = left_ref[...].T
    top, bottom = turned[:HALF], turned[HALF:]
    first = core_ref[0] == 0
    own = jnp.where(first, top, bottom)
    far = jnp.where(first, bottom, top)
    lhs_ref[0:HALF], lhs_ref[2 * HALF : 3 * HALF] = halves(own)
    lhs_ref[HALF : 2 * HALF], lhs_ref[3 * HALF :] = halves(far)
    columns = m_ref.shape[1]
    for start in range(0, columns, 256):
        stop = min(start + 256, columns)
        total = product(lhs_ref[...], m_ref[:, start:stop]) + product(lhs_ref[...], g_ref[:, start:stop])
        total = total[: 2 * HALF] + total[2 * HALF :]
        mine_ref[:, start:stop] = total[:HALF]
        other_ref[:, start:stop] = total[HALF:]


def cross_part(core, left, momentum, gradient):
    rows, columns = momentum.shape
    vmem = pl.BlockSpec(memory_space=pltpu.VMEM)
    return pl.pallas_call(
        cross_kernel,
        in_specs=[pl.BlockSpec(memory_space=pltpu.SMEM), vmem, vmem, vmem],
        out_specs=(vmem, vmem),
        out_shape=(jax.ShapeDtypeStruct((HALF, columns), jnp.float32),) * 2,
        scratch_shapes=[pltpu.VMEM((2 * RANK, rows), jnp.bfloat16)],
        compiler_params=params(24),
        cost_estimate=pl.CostEstimate(flops=1744830464, bytes_accessed=5600000, transcendentals=0),
        name="cross_part",
    )(core, left, momentum, gradient)


def right_kernel(core_ref, w_ref, mine_ref, other_ref, right_ref, squares_ref):
    w = w_ref[...]
    whole = jnp.zeros((RANK, HALF), jnp.float32)
    first = core_ref[0] == 0
    columns = mine_ref.shape[1]
    for start in range(0, columns, 256):
        stop = min(start + 256, columns)
        mine, other = mine_ref[:, start:stop], other_ref[:, start:stop]
        y = jnp.concatenate([jnp.where(first, mine, other), jnp.where(first, other, mine)], axis=0)
        right = dot_nn(w, y)
        right_ref[:, start:stop] = right
        square = right * right
        for k in range(0, stop - start, HALF):
            whole = whole + square[:, k : k + HALF]
    total = jnp.sum(whole.T, axis=0, keepdims=True)
    squares_ref[...] = jnp.broadcast_to(total[None], squares_ref.shape)


def right_part(core, w, mine, other):
    columns = mine.shape[1]
    vmem = pl.BlockSpec(memory_space=pltpu.VMEM)
    return pl.pallas_call(
        right_kernel,
        in_specs=[pl.BlockSpec(memory_space=pltpu.SMEM), vmem, vmem, vmem],
        out_specs=(vmem, vmem),
        out_shape=(
            jax.ShapeDtypeStruct((RANK, columns), jnp.float32),
            jax.ShapeDtypeStruct((16, 8, RANK), jnp.float32),
        ),
        compiler_params=params(40),
        cost_estimate=pl.CostEstimate(flops=1300000000, bytes_accessed=3400000, transcendentals=0),
        name="right_part",
    )(core, w, mine, other)


def low_rank(ortho, high_ref, low_ref, start, stop):
    count = ortho.shape[0] // 2
    total = product(ortho, high_ref[:, start:stop])
    return total[:count] + total[count:] + product(ortho[:count], low_ref[:, start:stop])


def momentum_kernel(
    m_ref, g_ref, left_ref, w_ref, right_ref, out_ref, turned_ref, high_ref, low_ref, ortho_ref
):
    columns = right_ref.shape[1]

    @pl.when(pl.program_id(0) == 0)
    def _():
        for start in range(0, columns, HALF):
            block = right_ref[:, start : start + HALF]
            high_ref[:, start : start + HALF], low_ref[:, start : start + HALF] = halves(block)
            turned_ref[start : start + HALF, :] = block.T

    ortho = dot_nt(left_ref[...], w_ref[...])
    ortho_ref[...] = ortho
    ortho = jnp.concatenate(halves(ortho), axis=0)
    for start in range(0, columns, 256):
        stop = min(start + 256, columns)
        buffer = m_ref[:, start:stop].astype(jnp.float32) + g_ref[:, start:stop].astype(jnp.float32)
        update = low_rank(ortho, high_ref, low_ref, start, stop)
        out_ref[:, start:stop] = (buffer - (1.0 - decay) * update).astype(jnp.bfloat16)


def momentum_part(momentum, gradient, left, w, right):
    rows, columns = momentum.shape
    step = rows // 2
    block = pl.BlockSpec((step, columns), lambda i: (i, 0))
    thin = pl.BlockSpec((step, RANK), lambda i: (i, 0))
    wide = pl.BlockSpec((RANK, columns), lambda i: (0, 0))
    return pl.pallas_call(
        momentum_kernel,
        grid=(2,),
        in_specs=[block, block, thin, pl.BlockSpec((RANK, RANK), lambda i: (0, 0)), wide],
        out_specs=(block, pl.BlockSpec((columns, RANK), lambda i: (0, 0)), wide, wide, thin),
        out_shape=(
            jax.ShapeDtypeStruct((rows, columns), jnp.bfloat16),
            jax.ShapeDtypeStruct((columns, RANK), jnp.float32),
            jax.ShapeDtypeStruct((RANK, columns), jnp.bfloat16),
            jax.ShapeDtypeStruct((RANK, columns), jnp.bfloat16),
            jax.ShapeDtypeStruct((rows, RANK), jnp.float32),
        ),
        compiler_params=params(60),
        cost_estimate=pl.CostEstimate(flops=1308622848, bytes_accessed=7500000, transcendentals=0),
        name="momentum_part",
    )(momentum, gradient, left, w, right)


def weight_kernel(squares_ref, weight_ref, ortho_ref, turned_ref, high_ref, low_ref, out_ref, factor_ref):
    squares = jnp.sum(squares_ref[...], axis=0)[0:1]
    scale = 1.0 / jnp.sqrt(squares / COLS + 1e-06)
    rate = step_size * (ROWS / RANK) ** 0.5
    ortho = jnp.concatenate(halves(ortho_ref[...] * (scale * rate)), axis=0)
    columns = high_ref.shape[1]
    for start in range(0, columns, 256):
        stop = min(start + 256, columns)
        update = low_rank(ortho, high_ref, low_ref, start, stop)
        out_ref[:, start:stop] = (weight_ref[:, start:stop].astype(jnp.float32) - update).astype(
            jnp.bfloat16
        )
    factor_ref[...] = turned_ref[...] * scale


def weight_part(squares, weight, ortho, turned, high, low):
    rows, columns = weight.shape
    step = rows // 2
    block = pl.BlockSpec((step, columns), lambda i: (i, 0))
    wide = pl.BlockSpec((RANK, columns), lambda i: (0, 0))
    factor = pl.BlockSpec((columns // 2, RANK), lambda i: (i, 0))
    return pl.pallas_call(
        weight_kernel,
        grid=(2,),
        in_specs=[
            pl.BlockSpec((16, 8, RANK), lambda i: (0, 0, 0)),
            block,
            pl.BlockSpec((step, RANK), lambda i: (i, 0)),
            factor,
            wide,
            wide,
        ],
        out_specs=(block, factor),
        out_shape=(
            jax.ShapeDtypeStruct((rows, columns), jnp.bfloat16),
            jax.ShapeDtypeStruct((columns, RANK), jnp.float32),
        ),
        compiler_params=params(60),
        cost_estimate=pl.CostEstimate(flops=1308622848, bytes_accessed=7500000, transcendentals=0),
        name="weight_part",
    )(squares, weight, ortho, turned, high, low)


def exchange(pieces, axis, groups=None):
    return lax.all_to_all(pieces, axis, 0, 0, axis_index_groups=groups)


def spread(piece, axis, count, groups=None):
    return exchange(jnp.broadcast_to(piece[None], (count,) + piece.shape), axis, groups)


def swap(value, axis, bits):
    return lax.ppermute(value, axis, [(i, i ^ bits) for i in range(16)])


def z_shift(k):
    return [(z * 2 + c, ((z + k) % 8) * 2 + c) for z in range(8) for c in range(2)]


def gather_near(piece, unit):
    return jnp.concatenate([piece] + [swap(piece, "col", k * unit) for k in (1, 2, 3)], axis=0)


def scatter_z(pieces, gram):
    z = lax.axis_index("row") // 2

    def own(k):
        return lax.dynamic_index_in_dim(pieces, (z + k) % 8, 0, keepdims=False)

    down, up = own(-4), own(3)
    for k, bits in enumerate((2, 4, 14)):
        down = lax.ppermute(down, "row", z_shift(-1)) + own(k - 3)
        up = lax.ppermute(up, "row", z_shift(1))
        up = up + own(2 - k)
        gram = gram + swap(gram, "row", bits)
        down, up, gram = lax.optimization_barrier((down, up, gram))
    gram = gather_near(gram[None], 1)
    total = up + lax.ppermute(down, "row", z_shift(-1))
    return lax.optimization_barrier((total, gram))


def local(gradient, momentum, weight, right_factor):
    core = (lax.axis_index("row") % 2).reshape(1)
    col = lax.axis_index("col")
    partial = left_part(momentum, gradient, right_factor)
    piece = jnp.sum(exchange(partial.reshape(16, 32, RANK), "col"), axis=0)
    left = spread(piece, "col", 16).reshape(512, RANK)
    gram = dot_tn(lax.dynamic_slice(left, (0, col * 16), (512, 16)), left)
    left, gram = lax.optimization_barrier((left, gram))
    gram = gram + swap(gram, "row", 1)
    mine, other = cross_part(core, left, momentum, gradient)
    mine = mine + lax.ppermute(other, "row", CORE_SWAP)
    mine, gram = lax.optimization_barrier((mine, gram))
    mine, gram = scatter_z(mine.reshape(8, 16, 1664), gram)
    gram = gather_near(gram, 4)
    mine = spread(mine, "row", 8, Z_GROUPS).reshape(HALF, 1664)
    jitter, first, gram = first_part(col.reshape(1), gram)
    inverse = second_part(jitter, first, gram)
    mine, inverse = lax.optimization_barrier((mine, inverse))
    other = lax.ppermute(mine, "row", CORE_SWAP)
    right, squares = right_part(core, inverse, mine, other)
    squares = exchange(squares, "col")
    new_momentum, turned, high, low, ortho = momentum_part(
        momentum, gradient, left, inverse, right
    )
    new_weight, new_factor = weight_part(squares, weight, ortho, turned, high, low)
    return (new_weight, new_momentum, new_factor)


def solution(mesh):
    in_specs = (P("row", "col"), P("row", "col"), P("row", "col"), P("col", None))
    out_specs = (P("row", "col"), P("row", "col"), P("col", None))
    return jax.shard_map(local, mesh=mesh, in_specs=in_specs, out_specs=out_specs, check_vma=False)
```
